512 devices in a mesh: pipe: 8 (over x, core), expert: 64 (over y, z).
Axes of the slice: x: 4, y: 8, z: 8, core: 2. Of those that a mesh axis runs over, the one named last changes fastest.
Arguments:
- fwd_tokens: bfloat16 [4096, 7168], P('expert', 'pipe'), may hold values from -6 to 6
- fwd_ids: int32 [4096, 8], P('expert'), may hold values from 0 to 63, all different within a row; in each aligned block of 64 rows (0 to 63, 64 to 127, ...) at most 10 rows name the same one
- fwd_gates: float32 [4096, 8], P('expert'), may hold values from 0.2 to 1
- bwd_tokens: bfloat16 [4096, 7168], P('expert', 'pipe'), may hold values from -6 to 6
- bwd_ids: int32 [4096, 8], P('expert'), may hold values from 0 to 63, all different within a row; in each aligned block of 64 rows (0 to 63, 64 to 127, ...) at most 10 rows name the same one
- bwd_gates: float32 [4096, 8], P('expert'), may hold values from 0.2 to 1
- bwd_cotangent: bfloat16 [4096, 7168], P('expert', 'pipe'), may hold values from -6 to 6
- w_up: bfloat16 [64, 7168, 1024], P('expert', 'pipe'), may hold values from -0.0625 to 0.0625
- w_down: bfloat16 [64, 1024, 7168], P('expert', None, 'pipe'), may hold values from -0.1875 to 0.1875
Outputs:
- fwd_out: bfloat16 [4096, 7168], P('expert', 'pipe')
- grad_in: bfloat16 [4096, 7168], P('expert', 'pipe')
The draws below stay inside these ranges and needn't reach their ends.
Inputs may be any that keep to these rules, and one draw needn't show every extreme that they name: `fwd_ids`: in the 64 rows of one device no expert is named by more than 10 rows, a bound that some block reaches; a row names 8 different experts. `bwd_ids`: in the 64 rows of one device no expert is named by more than 10 rows, a bound that some block reaches; a row names 8 different experts.
All inputs are finite; a program needn't handle non-finite values.
Results may differ from the reference program's by a relative error of at most 0.025.
Values may be sent and summed in bfloat16 or wider, within the bound.
A program may use at most 64 MiB of HBM per device.

```python
import math
import jax
import jax.numpy as jnp
import numpy as np
from jax import lax

D = 7168
TOP = 8
FF = 1024
TOK_DEV = 64
EXPERTS = 64
CAP = 10
SLOTS = 640
TOKENS = 4096
N_PIPE = 8
N_EXPERT = 64


def block_levels(key, dims, pieces, low, high):
    loudness, own = 1.0, jax.random.fold_in(key, 6)
    for axis_at, blocks in pieces:
        draws = jnp.exp(jax.random.uniform(jax.random.fold_in(own, axis_at), (blocks,), jnp.float32, low / len(pieces), high / len(pieces)))
        loudness = loudness * jnp.repeat(draws, dims[axis_at] // blocks).reshape([-1 if axis == axis_at else 1 for axis in range(len(dims))])
    return loudness


def shared_out(rng, own, number, rows, amount, top, limit, lean):
    ranking = jax.random.permutation(rng, amount)
    crowded, ordinary = load_shares(amount, rows * top, limit, lean, True), load_shares(amount, rows * top, limit, lean, False)
    places = jnp.arange(amount)

    def named(tallies, rotation):
        used = int((tallies > 0).sum())
        fixed = max(1, used // 4)
        shifted = fixed + (places - fixed + rotation * (used - fixed)) % max(1, amount - fixed)
        return jnp.zeros((amount,), jnp.int32).at[ranking[jnp.where(places < fixed, places, shifted)]].set(jnp.asarray(tallies, jnp.int32))

    tallies = jnp.where(number % 4 == 0, named(crowded, number // 4), named(ordinary, number - number // 4 - 1))
    mixed = jax.random.permutation(jax.random.fold_in(own, 3), amount)
    giver, taker = mixed[0:amount // 2 * 2:2], mixed[1:amount // 2 * 2:2]
    room = jnp.minimum(tallies[giver] - 1, limit - tallies[taker]) // 2
    room = jnp.where((giver == ranking[0]) | (taker == ranking[0]) | (tallies[taker] == 0), 0, jnp.maximum(room, 0))
    shifted = jax.random.randint(jax.random.fold_in(own, 4), (amount // 2,), 0, 1 << 20) % (room + 1)
    tallies = tallies.at[giver].add(-shifted).at[taker].add(shifted)
    members = jnp.searchsorted(jnp.cumsum(tallies), jnp.arange(rows * top), side="right").astype(jnp.int32)
    table = members.reshape(top, rows).T
    table = table[jax.random.permutation(jax.random.fold_in(own, 1), rows)]
    rotation = jax.random.randint(jax.random.fold_in(own, 2), (rows, 1), 0, top)
    return jnp.take_along_axis(table, (jnp.arange(top)[None, :] + rotation) % top, axis=1)


def load_shares(count, total, limit, skew, full):
    portions = [(1 << 20) // math.isqrt(rank ** skew) + 1 for rank in range(1, count + 1)]
    largest = limit if full else min(limit, max(-(-total // count), total * portions[0] // sum(portions)))
    least = 1 if total - largest >= count - 1 else 0
    given, surplus = [largest] + [least] * (count - 1), total - largest - least * (count - 1)
    while surplus > 0:
        movable = [i for i in range(1, count) if given[i] < largest] or [i for i in range(1, count) if given[i] < limit]
        mass, remaining = sum([portions[i] for i in movable]), surplus
        for i in movable:
            extra = min(limit - given[i], max(1, remaining * portions[i] // mass), surplus)
            given[i] = given[i] + extra
            surplus = surplus - extra
    return np.array(given)


def gaussian(stream_key, shape, deviation, bound, pieces=(), held_as=jnp.bfloat16):
    array = deviation * jax.random.normal(stream_key, shape, jnp.float32)
    if pieces:
        array = array * block_levels(stream_key, shape, pieces, -0.22, 0.18)
    return jnp.clip(array, -bound, bound).astype(held_as)


def setup_inputs(seed: int = 0) -> dict:
    splits = jax.random.split(jax.random.key(seed), 10)
    fwd_tokens = gaussian(splits[0], (TOKENS, D), 1.0, 6.0, ((0, 64), (1, 8)))
    fwd_ids_keys = jax.random.split(jax.random.fold_in(splits[1], 1), TOKENS // TOK_DEV)
    fwd_ids_turns = jax.random.permutation(jax.random.fold_in(splits[1], 3), TOKENS // TOK_DEV)
    fwd_ids = jax.vmap(lambda own, number: shared_out(jax.random.fold_in(splits[1], 2), own, number, TOK_DEV, EXPERTS, TOP, CAP, 2))(fwd_ids_keys, fwd_ids_turns).reshape((TOKENS, TOP))
    fwd_gates = jnp.clip(0.2 + 0.8 * jax.random.uniform(splits[2], (TOKENS, TOP), jnp.float32) ** block_levels(splits[2], (TOKENS, TOP), ((0, 64),), -0.2, 0.2), 0.2, 1.0)
    bwd_tokens = gaussian(splits[3], (TOKENS, D), 1.0, 6.0, ((0, 64), (1, 8)))
    bwd_ids_keys = jax.random.split(jax.random.fold_in(splits[4], 1), TOKENS // TOK_DEV)
    bwd_ids_turns = jax.random.permutation(jax.random.fold_in(splits[4], 3), TOKENS // TOK_DEV)
    bwd_ids = jax.vmap(lambda own, number: shared_out(jax.random.fold_in(splits[4], 2), own, number, TOK_DEV, EXPERTS, TOP, CAP, 2))(bwd_ids_keys, bwd_ids_turns).reshape((TOKENS, TOP))
    bwd_gates = jnp.clip(0.2 + 0.8 * jax.random.uniform(splits[5], (TOKENS, TOP), jnp.float32) ** block_levels(splits[5], (TOKENS, TOP), ((0, 64),), -0.2, 0.2), 0.2, 1.0)
    bwd_cotangent = gaussian(splits[6], (TOKENS, D), 1.0, 6.0, ((0, 64), (1, 8)))
    w_up = gaussian(splits[7], (EXPERTS, D, FF), D ** -0.5, 0.0625, ((0, 64), (1, 8)))
    w_down = gaussian(splits[8], (EXPERTS, FF, D), FF ** -0.5, 0.1875, ((0, 64), (2, 8)))
    return {"fwd_tokens": fwd_tokens, "fwd_ids": fwd_ids, "fwd_gates": fwd_gates, "bwd_tokens": bwd_tokens, "bwd_ids": bwd_ids, "bwd_gates": bwd_gates, "bwd_cotangent": bwd_cotangent, "w_up": w_up, "w_down": w_down}


def slot_index(ids):
    flat_ids = ids.reshape(N_EXPERT, TOK_DEV * TOP)
    labels = jnp.arange(EXPERTS, dtype=jnp.int32)
    onehot = (flat_ids[:, :, None] == labels[None, None, :]).astype(jnp.int32)
    rank_in = jnp.sum((jnp.cumsum(onehot, axis=1) - 1) * onehot, axis=2)
    blocks = jnp.arange(N_EXPERT, dtype=jnp.int32)[:, None]
    return (blocks * CAP + rank_in).reshape(TOKENS, TOP).astype(jnp.int32)


def owner_table(ids, slots):
    owners = jnp.repeat(jnp.arange(TOKENS, dtype=jnp.int32), TOP)
    table = jnp.full((EXPERTS, SLOTS), TOKENS, jnp.int32)
    return table.at[ids.reshape(-1), slots.reshape(-1)].set(owners)


def grouped_sum(left, right_of):
    width = D // N_PIPE
    total = jnp.zeros((left.shape[0], FF), jnp.float32)
    for index in range(N_PIPE):
        part = jnp.dot(left[:, index * width:(index + 1) * width], right_of(index * width, (index + 1) * width),
                       preferred_element_type=jnp.float32).astype(jnp.bfloat16)
        total = total + part.astype(jnp.float32)
    return total


def expert_forward(rows, up_proj, down_proj):
    pre_act = grouped_sum(rows, lambda lo, hi: up_proj[lo:hi])
    act_out = jax.nn.silu(pre_act).astype(jnp.bfloat16)
    return jnp.dot(act_out, down_proj, preferred_element_type=jnp.float32).astype(jnp.bfloat16)


def expert_backward(rows, grads, up_proj, down_proj):
    pre_act = grouped_sum(rows, lambda lo, hi: up_proj[lo:hi])
    dact = grouped_sum(grads, lambda lo, hi: down_proj[:, lo:hi].T)
    sigma = jax.nn.sigmoid(pre_act)
    dpre = (dact * sigma * (1.0 + pre_act * (1.0 - sigma))).astype(jnp.bfloat16)
    return jnp.dot(dpre, up_proj.T, preferred_element_type=jnp.float32).astype(jnp.bfloat16)


def combine(results, ids, slots, gates):
    picked = results[ids, slots].astype(jnp.float32)
    return jnp.sum(gates[:, :, None] * picked, axis=1).astype(jnp.bfloat16)


def reference(fwd_tokens, fwd_ids, fwd_gates, bwd_tokens, bwd_ids, bwd_gates, bwd_cotangent, w_up, w_down):
    blank = jnp.zeros((1, D), jnp.bfloat16)
    fwd_slot = slot_index(fwd_ids)
    fwd_table = owner_table(fwd_ids, fwd_slot)
    fwd_padded = jnp.concatenate([fwd_tokens, blank], axis=0)

    def forward_one(item):
        table_row, up_proj, down_proj = item
        return expert_forward(fwd_padded[table_row], up_proj, down_proj)

    fwd_results = lax.map(forward_one, (fwd_table, w_up, w_down))
    fwd_out = combine(fwd_results, fwd_ids, fwd_slot, fwd_gates)

    bwd_slot = slot_index(bwd_ids)
    bwd_table = owner_table(bwd_ids, bwd_slot)
    bwd_padded = jnp.concatenate([bwd_tokens, blank], axis=0)
    grad_padded = jnp.concatenate([bwd_cotangent, blank], axis=0)

    def backward_one(item):
        table_row, up_proj, down_proj = item
        return expert_backward(bwd_padded[table_row], grad_padded[table_row], up_proj, down_proj)

    bwd_results = lax.map(backward_one, (bwd_table, w_up, w_down))
    grad_in = combine(bwd_results, bwd_ids, bwd_slot, bwd_gates)
    return fwd_out, grad_in
```

```python
import functools
import math

import jax
import jax.numpy as jnp
from jax import lax
from jax.experimental import pallas as pl
from jax.experimental.pallas import tpu as pltpu
from jax.sharding import PartitionSpec as P

MESH = pl.DeviceIdType.MESH
F32 = jnp.float32
BF16 = jnp.bfloat16
NN = (((1,), (0,)), ((), ()))
NT = (((1,), (1,)), ((), ()))
TN = (((0,), (0,)), ((), ()))


def dot(left, right, dims=NN):
    return lax.dot_general(left, right, dims, preferred_element_type=F32)


def column_tiles(width, tile, body):
    whole = width // tile

    def step(index, carry):
        body(pl.multiple_of(index * tile, tile), tile)
        return carry

    if whole:
        lax.fori_loop(0, whole, step, 0)
    if width % tile:
        body(whole * tile, width % tile)


def kernel(
    side, nx, chunks, tile,
    ft, fi, fg, bt, bi, bg, bc, wu_hbm, wd_hbm,
    fwd_out, grad_out,
    wu, wd, ids, ids_t, info_own, info_all, slots, sel, gsel, perm,
    gathered, sending, arrived, kept, pair_tmp, pair_out, pair_in, xsend, xrecv,
    act, res_acc, res, returned, partial, part_send, part_recv,
    lsem, info_s, info_r, gat_s, gat_r, a2a_s, a2a_r, pr1_s, pr1_r, xrs_s, xrs_r,
    xag_s, xag_r, pr2_s, pr2_r, ret_s, ret_r, red_s, red_r,
):
    tok = ft.shape[0]
    half = wu.shape[1] // 2
    p = lax.axis_index("pipe")
    e = lax.axis_index("expert")
    x, c = p // 2, p % 2
    y, z = e // side, e % side
    j = z + c * (y - z)
    m = y + c * (z - y)
    sj = 1 + c * (side - 1)
    sm = side - c * (side - 1)

    def around(place, step, size):
        return (place + step) % size

    def gather_dev(place):
        return (p, place * sj + m * sm)

    def row_dev(place):
        return (p, j * sj + place * sm)

    def x_dev(place):
        return (place * 2 + c, e)

    core_dev = (x * 2 + 1 - c, e)

    def loop(start, stop, body):
        def step(index, carry):
            body(index)
            return carry

        lax.fori_loop(start, stop, step, 0)

    def remote(src, dst, ssem, rsem, device):
        return pltpu.make_async_remote_copy(
            src_ref=src, dst_ref=dst, send_sem=ssem, recv_sem=rsem,
            device_id=device, device_id_type=MESH,
        )

    tokens = (ft, bt, bc)
    route_of = (0, 1, 1)

    def own_block(q):
        return pltpu.make_async_copy(tokens[q], gathered.at[q, pl.ds(j * tok, tok)], lsem.at[q])

    load_up = pltpu.make_async_copy(wu_hbm, wu, lsem.at[3])
    load_down = pltpu.make_async_copy(wd_hbm, wd, lsem.at[4])
    for q in range(3):
        own_block(q).start()
    load_up.start()
    load_down.start()

    barrier = pltpu.get_barrier_semaphore()
    for step in range(1, side):
        pl.semaphore_signal(barrier, inc=1, device_id=gather_dev(around(j, step, side)), device_id_type=MESH)
        pl.semaphore_signal(barrier, inc=1, device_id=row_dev(around(m, step, side)), device_id_type=MESH)
    for step in range(1, nx):
        pl.semaphore_signal(barrier, inc=1, device_id=x_dev(around(x, step, nx)), device_id_type=MESH)
    pl.semaphore_signal(barrier, inc=1, device_id=core_dev, device_id_type=MESH)
    pl.semaphore_wait(barrier, 2 * (side - 1) + nx)

    def gather_copy(q, k):
        here = gathered.at[q, pl.ds(j * tok, tok)]
        return remote(tokens[q], here, gat_s.at[q, k], gat_r.at[q, k], gather_dev(around(j, k, side)))

    def info_copy(r, k):
        there = around(j, k, side)
        return remote(
            info_own.at[r, pl.ds(there * side, side)], info_all.at[r, pl.ds(j * side, side)],
            info_s.at[r, k], info_r.at[r, k], gather_dev(there),
        )

    def rows_at(n, place):
        first, count = chunks[n]
        return pl.ds(pl.multiple_of(side * first + place * count, 16), count)

    def row_copy(q, n, k):
        there = around(m, k, side)
        return remote(
            sending.at[q, rows_at(n, there)], arrived.at[q, rows_at(n, m)],
            a2a_s.at[q, n, k], a2a_r.at[q, n, k], row_dev(there),
        )

    def return_copy(r, n, k):
        there = around(m, k, side)
        return remote(
            res.at[r, rows_at(n, there)], returned.at[r, rows_at(n, m)],
            ret_s.at[r, n, k], ret_r.at[r, n, k], row_dev(there),
        )

    def reduce_copy(r, k):
        there = around(j, k, side)
        return remote(
            part_send.at[r, pl.ds(there * tok, tok)], part_recv.at[r, pl.ds(j * tok, tok)],
            red_s.at[r, k], red_r.at[r, k], gather_dev(there),
        )

    def all_rows(n):
        first, count = chunks[n]
        return pl.ds(side * first, side * count)

    def share(n, place):
        first, count = chunks[n]
        size = side * count // nx
        return pl.ds(pl.multiple_of(side * first + place * size, 16), size)

    def pair_copy(q, n):
        return remote(
            pair_out.at[q, all_rows(n)], pair_in.at[q, all_rows(n)],
            pr1_s.at[q, n], pr1_r.at[q, n], core_dev,
        )

    def scatter_copy(q, n, k):
        there = around(x, k, nx)
        return remote(
            xsend.at[q, share(n, there)], xrecv.at[q, share(n, x)],
            xrs_s.at[q, n, k], xrs_r.at[q, n, k], x_dev(there),
        )

    def spread_copy(r, n, k):
        here = act.at[r, c, share(n, x)]
        return remote(here, here, xag_s.at[r, n, k], xag_r.at[r, n, k], x_dev(around(x, k, nx)))

    def pair_act_copy(r, n):
        here = act.at[r, c, all_rows(n)]
        return remote(here, here, pr2_s.at[r, n], pr2_r.at[r, n], core_dev)

    def start_ring(size, copy):
        loop(1, size, lambda k: copy(k).start())

    def await_ring(size, copy):
        loop(1, size, lambda k: copy(k).wait_recv())

    def drain_ring(size, copy):
        loop(1, size, lambda k: copy(k).wait_send())

    def start_gather(q):
        start_ring(side, functools.partial(gather_copy, q))

    def route_info():
        rows = ids.shape[0]
        ids[...] = jnp.zeros_like(ids)
        for at in (0, rows // 2):
            for place, ref in enumerate((fi, fg, bi, bg)):
                width = ref.shape[1]
                ids[at:at + tok, place * width:(place + 1) * width] = ref[...].astype(F32)
        ids_t[...] = ids[...].T
        top = fi.shape[1]
        shape = (side * side, 2 * tok)
        row = lax.broadcasted_iota(jnp.int32, shape, 0)
        lane = lax.broadcasted_iota(jnp.int32, shape, 1)
        expert = ((row // side) * sj + (row % side) * sm).astype(F32)
        wide = (2 * tok, 2 * tok)
        before = lax.broadcasted_iota(jnp.int32, wide, 0)
        after = lax.broadcasted_iota(jnp.int32, wide, 1)
        earlier = jnp.where((before < after) & (after < tok), 1.0, 0.0).astype(BF16)
        for r in range(2):
            named = jnp.zeros(shape, F32)
            gate = jnp.zeros(shape, F32)
            for k in range(top):
                at = 2 * top * r + k
                hit = ids_t[at:at + 1, :] == expert
                named = named + jnp.where(hit, 1.0, 0.0)
                gate = gate + jnp.where(hit, ids_t[at + top:at + top + 1, :], 0.0)
            rank = dot(named.astype(BF16), earlier)
            slot = jnp.where(named > 0.5, rank * side + j.astype(F32), -1.0)
            info_own[r] = jnp.where(lane < tok, slot, gate)
            here = pl.ds(j * side, side)
            info_all[r, here] = info_own[r, here]

    def build_select(r):
        await_ring(side, functools.partial(info_copy, r))
        for b in range(side):
            here = info_all[r, b * side:(b + 1) * side, :]
            slots[0, :, b * tok:(b + 1) * tok] = here[:, :tok]
            slots[1, :, b * tok:(b + 1) * tok] = here[:, tok:]
        for n, (first, count) in enumerate(chunks):
            def body(place):
                line = lax.broadcasted_iota(jnp.int32, (count, side * tok), 0) + first
                hit = slots[0, pl.ds(place, 1), :] == line.astype(F32)
                at = rows_at(n, place)
                sel[r, at] = jnp.where(hit, 1.0, 0.0).astype(BF16)
                gsel[r, at] = jnp.where(hit, slots[1, pl.ds(place, 1), :], 0.0).astype(BF16)

            loop(0, side, body)

    def build_perm():
        for n, (first, count) in enumerate(chunks):
            def body(place):
                shape = (count, side * count)
                line = lax.broadcasted_iota(jnp.int32, shape, 0)
                lane = lax.broadcasted_iota(jnp.int32, shape, 1)
                other = line % side
                source = other * count + (line - other) + place
                perm[rows_at(n, place), :side * count] = jnp.where(source == lane, 1.0, 0.0).astype(BF16)

            loop(0, side, body)

    def permuted(n, ref, start, size):
        first, count = chunks[n]
        matrix = perm[all_rows(n), :side * count]
        return dot(matrix, ref[:, pl.ds(start, size)]).astype(BF16)

    def await_gather(q):
        own_block(q).wait()
        await_ring(side, functools.partial(gather_copy, q))

    def dispatch(q, n):
        r = route_of[q]

        def body(start, size):
            at = pl.ds(start, size)
            sending[q, all_rows(n), at] = dot(sel[r, all_rows(n)], gathered[q, :, at]).astype(BF16)

        column_tiles(ft.shape[1], tile, body)
        start_ring(side, functools.partial(row_copy, q, n))
        here = rows_at(n, m)
        arrived[q, here] = sending[q, here]

    def project(q, n):
        await_ring(side, functools.partial(row_copy, q, n))
        rows = all_rows(n)

        def product(at, size):
            if q == 2:
                return dot(arrived[q, rows], wd[pl.ds(at, size), :], NT)
            return dot(arrived[q, rows], wu[:, pl.ds(at, size)])

        def theirs(start, size):
            at = pl.multiple_of((1 - c) * half + start, 128)
            pair_tmp[rows, pl.ds(start, size)] = product(at, size).astype(BF16)
            pair_out[q, rows, pl.ds(start, size)] = permuted(n, pair_tmp.at[rows], start, size)

        def ours(start, size):
            at = pl.multiple_of(c * half + start, 128)
            kept[q, rows, pl.ds(start, size)] = product(at, size)

        column_tiles(half, tile, theirs)
        pair_copy(q, n).start()
        column_tiles(half, tile, ours)

    def scatter(q, n):
        pair_copy(q, n).wait_recv()
        rows = all_rows(n)
        xsend[q, rows] = (kept[q, rows] + pair_in[q, rows].astype(F32)).astype(BF16)
        start_ring(nx, functools.partial(scatter_copy, q, n))

    def summed(q, n):
        await_ring(nx, functools.partial(scatter_copy, q, n))
        total = xsend[q, share(n, x)].astype(F32)
        for k in range(1, nx):
            total = total + xrecv[q, share(n, around(x, k, nx))].astype(F32)
        return total

    def activate(r, n):
        if r == 0:
            pre = summed(0, n)
            value = pre / (1.0 + jnp.exp(-pre))
        else:
            pre = summed(1, n)
            grad = summed(2, n)
            sigma = 1.0 / (1.0 + jnp.exp(-pre))
            value = grad * sigma * (1.0 + pre * (1.0 - sigma))
        act[r, c, share(n, x)] = value.astype(BF16)
        start_ring(nx, functools.partial(spread_copy, r, n))

    def share_act(r, n):
        await_ring(nx, functools.partial(spread_copy, r, n))
        pair_act_copy(r, n).start()

    def expand(r, n):
        rows = all_rows(n)

        def product(left, start, at, size):
            if r == 0:
                return dot(left, wd[pl.ds(start, half), pl.ds(at, size)])
            return dot(left, wu[pl.ds(at, size), pl.ds(start, half)], NT)

        def ours(at, size):
            start = pl.multiple_of(c * half, 128)
            res_acc[rows, pl.ds(at, size)] = product(act[r, c, rows], start, at, size)

        column_tiles(ft.shape[1], tile, ours)
        pair_act_copy(r, n).wait_recv()

        def reorder(start, size):
            pair_tmp[rows, pl.ds(start, size)] = permuted(n, act.at[r, 1 - c, rows], start, size)

        column_tiles(half, tile, reorder)

        def theirs(at, size):
            start = pl.multiple_of((1 - c) * half, 128)
            here = pl.ds(at, size)
            total = res_acc[rows, here] + product(pair_tmp[rows], start, at, size)
            res[r, rows, here] = total.astype(BF16)

        column_tiles(ft.shape[1], tile, theirs)
        start_ring(side, functools.partial(return_copy, r, n))
        here = rows_at(n, m)
        returned[r, here] = res[r, here]

    def combine(r):
        for n in range(len(chunks)):
            await_ring(side, functools.partial(return_copy, r, n))

        def body(at, size):
            here = pl.ds(at, size)
            total = dot(gsel[r], returned[r, :, here], TN)
            partial[:, here] = total
            part_send[r, :, here] = total.astype(BF16)

        column_tiles(ft.shape[1], tile, body)
        start_ring(side, functools.partial(reduce_copy, r))
        part_recv_own = pl.ds(j * tok, tok)
        own[r] = partial[part_recv_own]

    def finish(r, out):
        await_ring(side, functools.partial(reduce_copy, r))
        total = own[r]
        for k in range(1, side):
            there = pl.ds(around(j, k, side) * tok, tok)
            total = total + part_recv[r, there].astype(F32)
        out[...] = total.astype(BF16)

    own = {}

    count = len(chunks)
    start_gather(0)
    route_info()
    for r in range(2):
        start_ring(side, functools.partial(info_copy, r))
    build_perm()
    build_select(0)
    await_gather(0)
    start_gather(1)
    for n in range(count):
        dispatch(0, n)
    build_select(1)
    await_gather(1)
    start_gather(2)
    for n in range(count):
        dispatch(1, n)
    load_up.wait()
    load_down.wait()
    for n in range(count):
        project(0, n)
    for n in range(count):
        scatter(0, n)
    await_gather(2)
    for n in range(count):
        dispatch(2, n)
    for n in range(count):
        activate(0, n)
    for n in range(count):
        project(1, n)
    for n in range(count):
        share_act(0, n)
    for n in range(count):
        scatter(1, n)
    for n in range(count):
        expand(0, n)
    for n in range(count):
        project(2, n)
    for n in range(count):
        scatter(2, n)
    for n in range(count):
        activate(1, n)
    combine(0)
    for n in range(count):
        share_act(1, n)
    for n in range(count):
        expand(1, n)
    finish(0, fwd_out)
    combine(1)
    finish(1, grad_out)

    for q in range(3):
        drain_ring(side, functools.partial(gather_copy, q))
        for n in range(count):
            drain_ring(side, functools.partial(row_copy, q, n))
            pair_copy(q, n).wait_send()
            drain_ring(nx, functools.partial(scatter_copy, q, n))
    for r in range(2):
        drain_ring(side, functools.partial(info_copy, r))
        drain_ring(side, functools.partial(reduce_copy, r))
        for n in range(count):
            drain_ring(nx, functools.partial(spread_copy, r, n))
            pair_act_copy(r, n).wait_send()
            drain_ring(side, functools.partial(return_copy, r, n))


def build(mesh, capacity, chunks, tile=256):
    n_pipe, n_expert = mesh.shape["pipe"], mesh.shape["expert"]
    side, nx = math.isqrt(n_expert), n_pipe // 2

    def local(ft, fi, fg, bt, bi, bg, bc, w_up, w_down):
        tok, width = ft.shape
        ff = w_up.shape[2]
        half = ff // 2
        rows = n_expert * capacity
        count = len(chunks)
        ring = side * tok
        dma = pltpu.SemaphoreType.DMA
        vmem = pltpu.VMEM
        widest = side * max(size for _, size in chunks)
        scratch = [
            vmem((width, ff), BF16), vmem((ff, width), BF16),
            vmem((2 * tok, 2 * tok), F32), vmem((2 * tok, 2 * tok), F32),
            vmem((2, n_expert, 2 * tok), F32), vmem((2, n_expert, 2 * tok), F32),
            vmem((2, side, ring), F32),
            vmem((2, rows, ring), BF16), vmem((2, rows, ring), BF16), vmem((rows, widest), BF16),
            vmem((3, ring, width), BF16), vmem((3, rows, width), BF16), vmem((3, rows, width), BF16),
            vmem((3, rows, half), F32), vmem((rows, half), BF16),
            vmem((3, rows, half), BF16), vmem((3, rows, half), BF16),
            vmem((3, rows, half), BF16), vmem((3, rows, half), BF16),
            vmem((2, 2, rows, half), BF16),
            vmem((rows, width), F32), vmem((2, rows, width), BF16), vmem((2, rows, width), BF16),
            vmem((ring, width), F32), vmem((2, ring, width), BF16), vmem((2, ring, width), BF16),
            dma((5,)), dma((2, side)), dma((2, side)), dma((3, side)), dma((3, side)),
            dma((3, count, side)), dma((3, count, side)), dma((3, count)), dma((3, count)),
            dma((3, count, nx)), dma((3, count, nx)), dma((2, count, nx)), dma((2, count, nx)),
            dma((2, count)), dma((2, count)), dma((2, count, side)), dma((2, count, side)),
            dma((2, side)), dma((2, side)),
        ]
        any_spec = pl.BlockSpec(memory_space=pl.ANY)
        vmem_spec = pl.BlockSpec(memory_space=pltpu.VMEM)
        out = jax.ShapeDtypeStruct((tok, width), BF16)
        return pl.pallas_call(
            functools.partial(kernel, side, nx, chunks, tile),
            out_shape=(out, out),
            in_specs=[any_spec, vmem_spec, vmem_spec, any_spec, vmem_spec, vmem_spec, any_spec, any_spec, any_spec],
            out_specs=(vmem_spec, vmem_spec),
            scratch_shapes=scratch,
            compiler_params=pltpu.CompilerParams(
                collective_id=0, has_side_effects=True, vmem_limit_bytes=60 * 2**20
            ),
            cost_estimate=pl.CostEstimate(flops=12 * rows * width * ff, bytes_accessed=6 * width * ff, transcendentals=0),
        )(ft, fi, fg, bt, bi, bg, bc, w_up[0], w_down[0])

    in_specs = (
        P("expert", "pipe"), P("expert", None), P("expert", None),
        P("expert", "pipe"), P("expert", None), P("expert", None),
        P("expert", "pipe"), P("expert", "pipe", None), P("expert", None, "pipe"),
    )
    out_specs = (P("expert", "pipe"), P("expert", "pipe"))
    return jax.shard_map(local, mesh=mesh, in_specs=in_specs, out_specs=out_specs, check_vma=False)


def solution(mesh):
    return build(mesh, 10, ((0, 48), (48, 32)))
```

```python
import functools
import math

import jax
import jax.numpy as jnp
from jax import lax
from jax.experimental import pallas as pl
from jax.experimental.pallas import tpu as pltpu
from jax.sharding import PartitionSpec as P

MESH = pl.DeviceIdType.MESH
F32 = jnp.float32
BF16 = jnp.bfloat16
NN = (((1,), (0,)), ((), ()))
NT = (((1,), (1,)), ((), ()))
TN = (((0,), (0,)), ((), ()))


def dot(left, right, dims=NN):
    return lax.dot_general(left, right, dims, preferred_element_type=F32)


def column_tiles(width, tile, body):
    whole = width // tile

    def step(index, carry):
        body(pl.multiple_of(index * tile, tile), tile)
        return carry

    if whole:
        lax.fori_loop(0, whole, step, 0)
    if width % tile:
        body(whole * tile, width % tile)


def kernel(
    side, nx, chunks, tile,
    ft, fi, fg, bt, bi, bg, bc, wu_hbm, wd_hbm,
    fwd_out, grad_out,
    wu, wd, ids, gates, info_own, info_all, slots, sel, gsel, perm,
    gathered, sending, arrived, kept, pair_tmp, pair_out, pair_in, xsend, xrecv,
    act, res_acc, res, returned, partial, part_send, part_recv, fold,
    lsem, info_s, info_r, gat_s, gat_r, a2a_s, a2a_r, pr1_s, pr1_r, xrs_s, xrs_r,
    xag_s, xag_r, pr2_s, pr2_r, ret_s, ret_r, red_s, red_r,
):
    tok = ft.shape[0]
    part = tok // 2
    half = wu.shape[1] // 2
    p = lax.axis_index("pipe")
    e = lax.axis_index("expert")
    x, c = p // 2, p % 2
    y, z = e // side, e % side
    j = z + c * (y - z)
    m = y + c * (z - y)
    sj = 1 + c * (side - 1)
    sm = side - c * (side - 1)

    def around(place, step, size):
        return (place + step) % size

    def gather_dev(place):
        return (p, place * sj + m * sm)

    def row_dev(place):
        return (p, j * sj + place * sm)

    def x_dev(place):
        return (place * 2 + c, e)

    core_dev = (x * 2 + 1 - c, e)

    def loop(start, stop, body):
        def step(index, carry):
            body(index)
            return carry

        lax.fori_loop(start, stop, step, 0)

    def remote(src, dst, ssem, rsem, device):
        return pltpu.make_async_remote_copy(
            src_ref=src, dst_ref=dst, send_sem=ssem, recv_sem=rsem,
            device_id=device, device_id_type=MESH,
        )

    tokens = (ft, bt, bc)
    route_of = (0, 1, 1)

    def own_block(q):
        return pltpu.make_async_copy(tokens[q], gathered.at[q, pl.ds(j * tok, tok)], lsem.at[q])

    load_up = pltpu.make_async_copy(wu_hbm, wu, lsem.at[3])
    load_down = pltpu.make_async_copy(wd_hbm, wd, lsem.at[4])
    for q in range(3):
        own_block(q).start()
    small = tuple(
        pltpu.make_async_copy(ref, into, lsem.at[5 + at])
        for at, (ref, into) in enumerate(((fi, ids.at[0]), (fg, gates.at[0]), (bi, ids.at[1]), (bg, gates.at[1])))
    )
    for copy in small:
        copy.start()
    load_up.start()
    load_down.start()

    barrier = pltpu.get_barrier_semaphore()
    for step in range(1, side):
        pl.semaphore_signal(barrier, inc=1, device_id=gather_dev(around(j, step, side)), device_id_type=MESH)
        pl.semaphore_signal(barrier, inc=1, device_id=row_dev(around(m, step, side)), device_id_type=MESH)
    for step in range(1, nx):
        pl.semaphore_signal(barrier, inc=1, device_id=x_dev(around(x, step, nx)), device_id_type=MESH)
    pl.semaphore_signal(barrier, inc=1, device_id=core_dev, device_id_type=MESH)
    pl.semaphore_wait(barrier, 2 * (side - 1) + nx)

    def block(place):
        return pl.ds(pl.multiple_of(place * tok, tok), tok)

    GATHER = (
        (0, 1, None), (0, -1, None), (0, 2, None), (0, -2, None),
        (-2, 1, None), (2, -1, None), (-2, 2, 0), (2, -2, 1),
    )

    def gather_copy(q, kind):
        origin, target, piece = GATHER[kind]
        place = around(j, side + origin, side)
        rows = block(place)
        if piece is not None:
            rows = pl.ds(pl.multiple_of(place * tok + piece * part, part), part)
        here = gathered.at[q, rows]
        source = tokens[q] if origin == 0 else here
        return remote(source, here, gat_s.at[q, kind], gat_r.at[q, kind], gather_dev(around(j, side + target, side)))

    def info_copy(r, k):
        there = around(j, k, side)
        return remote(
            info_own.at[r, pl.ds(there * side, side)], info_all.at[r, pl.ds(j * side, side)],
            info_s.at[r, k], info_r.at[r, k], gather_dev(there),
        )

    def rows_at(n, place):
        first, count = chunks[n]
        return pl.ds(pl.multiple_of(side * first + place * count, 16), count)

    def row_copy(q, n, k):
        there = around(m, k, side)
        return remote(
            sending.at[q, rows_at(n, there)], arrived.at[q, rows_at(n, m)],
            a2a_s.at[q, n, k], a2a_r.at[q, n, k], row_dev(there),
        )

    def return_copy(r, n, k):
        there = around(m, k, side)
        return remote(
            res.at[r, rows_at(n, there)], returned.at[r, rows_at(n, m)],
            ret_s.at[r, n, k], ret_r.at[r, n, k], row_dev(there),
        )

    REDUCE = (
        (1, 1, None), (-1, -1, None), (3, 1, None), (-3, -1, None),
        (4, 2, 1), (4, -2, 0), (2, 2, None), (-2, -2, None),
    )

    def reduce_copy(r, kind):
        owner, target, piece = REDUCE[kind]
        place = around(j, side + owner, side)
        source, there = part_send.at[r, block(place)], part_recv.at[r, kind]
        if kind >= 6:
            source = fold.at[r, kind - 6]
        if piece is not None:
            source = part_send.at[r, pl.ds(pl.multiple_of(place * tok + piece * part, part), part)]
            there = part_recv.at[r, kind, pl.ds(piece * part, part)]
        return remote(source, there, red_s.at[r, kind], red_r.at[r, kind], gather_dev(around(j, side + target, side)))

    def all_rows(n):
        first, count = chunks[n]
        return pl.ds(side * first, side * count)

    def share(n, place):
        first, count = chunks[n]
        size = side * count // nx
        return pl.ds(pl.multiple_of(side * first + place * size, 16), size)

    def pair_copy(q, n):
        return remote(
            pair_out.at[q, all_rows(n)], pair_in.at[q, all_rows(n)],
            pr1_s.at[q, n], pr1_r.at[q, n], core_dev,
        )

    def scatter_copy(q, n, k):
        there = around(x, k, nx)
        return remote(
            xsend.at[q, share(n, there)], xrecv.at[q, share(n, x)],
            xrs_s.at[q, n, k], xrs_r.at[q, n, k], x_dev(there),
        )

    def spread_copy(r, n, k):
        here = act.at[r, c, share(n, x)]
        return remote(here, here, xag_s.at[r, n, k], xag_r.at[r, n, k], x_dev(around(x, k, nx)))

    def pair_act_copy(r, n):
        here = act.at[r, c, all_rows(n)]
        return remote(here, here, pr2_s.at[r, n], pr2_r.at[r, n], core_dev)

    def start_ring(size, copy):
        loop(1, size, lambda k: copy(k).start())

    def await_ring(size, copy):
        loop(1, size, lambda k: copy(k).wait_recv())

    def drain_ring(size, copy):
        loop(1, size, lambda k: copy(k).wait_send())

    def start_gather(q):
        for kind in (2, 3, 0, 1):
            gather_copy(q, kind).start()

    def pass_on(q):
        for kind in (2, 3):
            gather_copy(q, kind).wait_recv()
            gather_copy(q, kind + 4).start()
            gather_copy(q, kind + 2).start()

    def route_info():
        for copy in small:
            copy.wait()
        shape = (side * side, 2 * tok)
        row = lax.broadcasted_iota(jnp.int32, shape, 0)
        lane = lax.broadcasted_iota(jnp.int32, shape, 1)
        expert = (row // side) * sj + (row % side) * sm
        wide = (2 * tok, 2 * tok)
        before = lax.broadcasted_iota(jnp.int32, wide, 0)
        after = lax.broadcasted_iota(jnp.int32, wide, 1)
        earlier = jnp.where((before < after) & (after < tok), 1.0, 0.0).astype(BF16)
        for r in range(2):
            names = jnp.concatenate([ids[r], ids[r]], axis=1)
            weights = jnp.concatenate([gates[r], gates[r]], axis=1)
            named = jnp.zeros(shape, F32)
            gate = jnp.zeros(shape, F32)
            for k in range(ids.shape[1]):
                hit = names[k:k + 1, :] == expert
                named = named + jnp.where(hit, 1.0, 0.0)
                gate = gate + jnp.where(hit, weights[k:k + 1, :], 0.0)
            rank = dot(named.astype(BF16), earlier)
            slot = jnp.where(named > 0.5, rank * side + j.astype(F32), -1.0)
            info_own[r] = jnp.where(lane < tok, slot, gate)
            here = pl.ds(pl.multiple_of(j * side, side), side)
            info_all[r, here] = info_own[r, here]
            start_ring(side, functools.partial(info_copy, r))

    def build_select(r):
        await_ring(side, functools.partial(info_copy, r))
        for b in range(side):
            here = info_all[r, b * side:(b + 1) * side, :]
            slots[0, :, b * tok:(b + 1) * tok] = here[:, :tok]
            slots[1, :, b * tok:(b + 1) * tok] = here[:, tok:]
        for n, (first, count) in enumerate(chunks):
            def body(place):
                line = lax.broadcasted_iota(jnp.int32, (count, side * tok), 0) + first
                hit = slots[0, pl.ds(place, 1), :] == line.astype(F32)
                at = rows_at(n, place)
                sel[r, at] = jnp.where(hit, 1.0, 0.0).astype(BF16)
                gsel[r, at] = jnp.where(hit, slots[1, pl.ds(place, 1), :], 0.0).astype(BF16)

            loop(0, side, body)

    def build_perm():
        for n, (first, count) in enumerate(chunks):
            def body(place):
                shape = (count, side * count)
                line = lax.broadcasted_iota(jnp.int32, shape, 0)
                lane = lax.broadcasted_iota(jnp.int32, shape, 1)
                other = line % side
                source = other * count + (line - other) + place
                perm[rows_at(n, place), :side * count] = jnp.where(source == lane, 1.0, 0.0).astype(BF16)

            loop(0, side, body)

    def permuted(n, ref, start, size):
        first, count = chunks[n]
        matrix = perm[all_rows(n), :side * count]
        return dot(matrix, ref[:, pl.ds(start, size)]).astype(BF16)

    def await_gather(q):
        own_block(q).wait()
        for kind in (0, 1, 4, 5, 6, 7):
            gather_copy(q, kind).wait_recv()

    def dispatch(q, n):
        r = route_of[q]

        def body(start, size):
            at = pl.ds(start, size)
            sending[q, all_rows(n), at] = dot(sel[r, all_rows(n)], gathered[q, :, at]).astype(BF16)

        column_tiles(ft.shape[1], tile, body)
        start_ring(side, functools.partial(row_copy, q, n))
        here = rows_at(n, m)
        arrived[q, here] = sending[q, here]

    def project(q, n):
        await_ring(side, functools.partial(row_copy, q, n))
        rows = all_rows(n)

        def product(at, size):
            if q == 2:
                return dot(arrived[q, rows], wd[pl.ds(at, size), :], NT)
            return dot(arrived[q, rows], wu[:, pl.ds(at, size)])

        def theirs(start, size):
            at = pl.multiple_of((1 - c) * half + start, 128)
            pair_tmp[rows, pl.ds(start, size)] = product(at, size).astype(BF16)
            pair_out[q, rows, pl.ds(start, size)] = permuted(n, pair_tmp.at[rows], start, size)

        def ours(start, size):
            at = pl.multiple_of(c * half + start, 128)
            kept[q, rows, pl.ds(start, size)] = product(at, size)

        column_tiles(half, tile, theirs)
        pair_copy(q, n).start()
        column_tiles(half, tile, ours)

    def scatter(q, n):
        pair_copy(q, n).wait_recv()
        rows = all_rows(n)
        xsend[q, rows] = (kept[q, rows] + pair_in[q, rows].astype(F32)).astype(BF16)
        start_ring(nx, functools.partial(scatter_copy, q, n))

    def summed(q, n):
        await_ring(nx, functools.partial(scatter_copy, q, n))
        total = xsend[q, share(n, x)].astype(F32)
        for k in range(1, nx):
            total = total + xrecv[q, share(n, around(x, k, nx))].astype(F32)
        return total

    def activate(r, n):
        if r == 0:
            pre = summed(0, n)
            value = pre / (1.0 + jnp.exp(-pre))
        else:
            pre = summed(1, n)
            grad = summed(2, n)
            sigma = 1.0 / (1.0 + jnp.exp(-pre))
            value = grad * sigma * (1.0 + pre * (1.0 - sigma))
        act[r, c, share(n, x)] = value.astype(BF16)
        start_ring(nx, functools.partial(spread_copy, r, n))

    def share_act(r, n):
        await_ring(nx, functools.partial(spread_copy, r, n))
        pair_act_copy(r, n).start()

    def expand(r, n):
        rows = all_rows(n)

        def product(left, start, at, size):
            if r == 0:
                return dot(left, wd[pl.ds(start, half), pl.ds(at, size)])
            return dot(left, wu[pl.ds(at, size), pl.ds(start, half)], NT)

        def ours(at, size):
            start = pl.multiple_of(c * half, 128)
            res_acc[rows, pl.ds(at, size)] = product(act[r, c, rows], start, at, size)

        column_tiles(ft.shape[1], tile, ours)
        pair_act_copy(r, n).wait_recv()

        def reorder(start, size):
            pair_tmp[rows, pl.ds(start, size)] = permuted(n, act.at[r, 1 - c, rows], start, size)

        column_tiles(half, tile, reorder)

        def theirs(at, size):
            start = pl.multiple_of((1 - c) * half, 128)
            here = pl.ds(at, size)
            total = res_acc[rows, here] + product(pair_tmp[rows], start, at, size)
            res[r, rows, here] = total.astype(BF16)

        column_tiles(ft.shape[1], tile, theirs)
        start_ring(side, functools.partial(return_copy, r, n))
        here = rows_at(n, m)
        returned[r, here] = res[r, here]

    def combine(r, n):
        await_ring(side, functools.partial(return_copy, r, n))
        rows = all_rows(n)
        last = n == len(chunks) - 1

        def body(at, size):
            here = pl.ds(at, size)
            total = dot(gsel[r, rows], returned[r, rows, here], TN)
            if n:
                total = total + partial[r, :, here]
            partial[r, :, here] = total
            if last:
                part_send[r, :, here] = total.astype(BF16)

        column_tiles(ft.shape[1], tile, body)
        if last:
            for kind in (4, 5, 2, 3, 0, 1):
                reduce_copy(r, kind).start()

    def fold_in(r):
        for kind in (2, 3, 4, 5):
            reduce_copy(r, kind).wait_recv()
        for at, owner in enumerate((2, -2)):
            mine = block(around(j, side + owner, side))
            fold[r, at] = (partial[r, mine] + part_recv[r, 2 + at].astype(F32)).astype(BF16)
            piece = pl.ds((1 - at) * part, part)
            extra = pl.ds(pl.multiple_of(around(j, side + owner, side) * tok + (1 - at) * part, part), part)
            total = partial[r, extra] + part_recv[r, 2 + at, piece].astype(F32)
            fold[r, at, piece] = (total + part_recv[r, 4 + at, piece].astype(F32)).astype(BF16)
            reduce_copy(r, 6 + at).start()

    def finish(r, out):
        total = partial[r, block(j)]
        for kind in (0, 1, 6, 7):
            reduce_copy(r, kind).wait_recv()
            total = total + part_recv[r, kind].astype(F32)
        out[...] = total.astype(BF16)

    start_gather(0)
    start_gather(1)
    start_gather(2)
    route_info()
    build_perm()
    pass_on(0)
    pass_on(1)
    build_select(0)
    pass_on(2)
    build_select(1)
    await_gather(0)
    dispatch(0, 0)
    await_gather(1)
    dispatch(0, 1)
    dispatch(1, 0)
    await_gather(2)
    dispatch(2, 0)
    load_up.wait()
    load_down.wait()
    project(0, 0)
    scatter(0, 0)
    dispatch(1, 1)
    project(0, 1)
    scatter(0, 1)
    dispatch(2, 1)
    activate(0, 0)
    activate(0, 1)
    project(1, 0)
    scatter(1, 0)
    share_act(0, 0)
    share_act(0, 1)
    expand(0, 0)
    expand(0, 1)
    project(2, 0)
    scatter(2, 0)
    project(1, 1)
    scatter(1, 1)
    activate(1, 0)
    project(2, 1)
    scatter(2, 1)
    combine(0, 0)
    combine(0, 1)
    share_act(1, 0)
    expand(1, 0)
    activate(1, 1)
    share_act(1, 1)
    expand(1, 1)
    fold_in(0)
    combine(1, 0)
    combine(1, 1)
    finish(0, fwd_out)
    fold_in(1)
    finish(1, grad_out)

    for q in range(3):
        for kind in range(8):
            gather_copy(q, kind).wait_send()
        for n in range(len(chunks)):
            drain_ring(side, functools.partial(row_copy, q, n))
            pair_copy(q, n).wait_send()
            drain_ring(nx, functools.partial(scatter_copy, q, n))
    for r in range(2):
        drain_ring(side, functools.partial(info_copy, r))
        for kind in range(8):
            reduce_copy(r, kind).wait_send()
        for n in range(len(chunks)):
            drain_ring(nx, functools.partial(spread_copy, r, n))
            pair_act_copy(r, n).wait_send()
            drain_ring(side, functools.partial(return_copy, r, n))


def build(mesh, capacity, chunks, tile=256):
    n_pipe, n_expert = mesh.shape["pipe"], mesh.shape["expert"]
    side, nx = math.isqrt(n_expert), n_pipe // 2

    def local(ft, fi, fg, bt, bi, bg, bc, w_up, w_down):
        tok, width = ft.shape
        top = fi.shape[1]
        ff = w_up.shape[2]
        half = ff // 2
        rows = n_expert * capacity
        count = len(chunks)
        ring = side * tok
        dma = pltpu.SemaphoreType.DMA
        vmem = pltpu.VMEM
        widest = side * max(size for _, size in chunks)
        scratch = [
            vmem((width, ff), BF16), vmem((ff, width), BF16),
            vmem((2, top, tok), jnp.int32), vmem((2, top, tok), F32),
            vmem((2, n_expert, 2 * tok), F32), vmem((2, n_expert, 2 * tok), F32),
            vmem((2, side, ring), F32),
            vmem((2, rows, ring), BF16), vmem((2, rows, ring), BF16), vmem((rows, widest), BF16),
            vmem((3, ring, width), BF16), vmem((3, rows, width), BF16), vmem((3, rows, width), BF16),
            vmem((3, rows, half), F32), vmem((rows, half), BF16),
            vmem((3, rows, half), BF16), vmem((3, rows, half), BF16),
            vmem((3, rows, half), BF16), vmem((3, rows, half), BF16),
            vmem((2, 2, rows, half), BF16),
            vmem((rows, width), F32), vmem((2, rows, width), BF16), vmem((2, rows, width), BF16),
            vmem((2, ring, width), F32), vmem((2, ring, width), BF16), vmem((2, 8, tok, width), BF16),
            vmem((2, 2, tok, width), BF16),
            dma((9,)), dma((2, side)), dma((2, side)), dma((3, 8)), dma((3, 8)),
            dma((3, count, side)), dma((3, count, side)), dma((3, count)), dma((3, count)),
            dma((3, count, nx)), dma((3, count, nx)), dma((2, count, nx)), dma((2, count, nx)),
            dma((2, count)), dma((2, count)), dma((2, count, side)), dma((2, count, side)),
            dma((2, 8)), dma((2, 8)),
        ]
        any_spec = pl.BlockSpec(memory_space=pl.ANY)
        vmem_spec = pl.BlockSpec(memory_space=pltpu.VMEM)
        out = jax.ShapeDtypeStruct((tok, width), BF16)
        return pl.pallas_call(
            functools.partial(kernel, side, nx, chunks, tile),
            out_shape=(out, out),
            in_specs=[any_spec] * 9,
            out_specs=(vmem_spec, vmem_spec),
            scratch_shapes=scratch,
            compiler_params=pltpu.CompilerParams(
                collective_id=0, has_side_effects=True, vmem_limit_bytes=60 * 2**20
            ),
            cost_estimate=pl.CostEstimate(flops=12 * rows * width * ff, bytes_accessed=6 * width * ff, transcendentals=0),
        )(ft, fi.T, fg.T, bt, bi.T, bg.T, bc, w_up[0], w_down[0])

    in_specs = (
        P("expert", "pipe"), P("expert", None), P("expert", None),
        P("expert", "pipe"), P("expert", None), P("expert", None),
        P("expert", "pipe"), P("expert", "pipe", None), P("expert", None, "pipe"),
    )
    out_specs = (P("expert", "pipe"), P("expert", "pipe"))
    return jax.shard_map(local, mesh=mesh, in_specs=in_specs, out_specs=out_specs, check_vma=False)


def solution(mesh):
    return build(mesh, 10, ((0, 48), (48, 32)))
```

```python
import functools
import math

import jax
import jax.numpy as jnp
from jax import lax
from jax.experimental import pallas as pl
from jax.experimental.pallas import tpu as pltpu
from jax.sharding import PartitionSpec as P

MESH = pl.DeviceIdType.MESH
F32 = jnp.float32
BF16 = jnp.bfloat16
NN = (((1,), (0,)), ((), ()))
NT = (((1,), (1,)), ((), ()))
TN = (((0,), (0,)), ((), ()))


def dot(left, right, dims=NN):
    return lax.dot_general(left, right, dims, preferred_element_type=F32)


def column_tiles(width, tile, body):
    whole = width // tile

    def step(index, carry):
        body(pl.multiple_of(index * tile, tile), tile)
        return carry

    if whole:
        lax.fori_loop(0, whole, step, 0)
    if width % tile:
        body(whole * tile, width % tile)


def kernel(
    side, nx, chunks, tile,
    ft, fi, fg, bt, bi, bg, bc, wu_hbm, wd_hbm,
    both_out,
    wu, wd, ids, gates, info_own, info_all, slots, sel, gsel, perm,
    gathered, sending, arrived, kept, pair_tmp, pair_out, pair_in, xsend, xrecv,
    act, res_acc, res, returned, partial, part_send, part_recv, fold, result,
    lsem, info_s, info_r, gat_s, gat_r, a2a_s, a2a_r, pr1_s, pr1_r, xrs_s, xrs_r,
    xag_s, xag_r, pr2_s, pr2_r, ret_s, ret_r, red_s, red_r,
):
    tok = ft.shape[0]
    part = tok // 2
    half = wu.shape[1] // 2
    p = lax.axis_index("pipe")
    e = lax.axis_index("expert")
    x, c = p // 2, p % 2
    y, z = e // side, e % side
    j = z + c * (y - z)
    m = y + c * (z - y)
    sj = 1 + c * (side - 1)
    sm = side - c * (side - 1)

    def around(place, step, size):
        return (place + step) % size

    def gather_dev(place):
        return (p, place * sj + m * sm)

    def row_dev(place):
        return (p, j * sj + place * sm)

    def x_dev(place):
        return (place * 2 + c, e)

    core_dev = (x * 2 + 1 - c, e)

    def loop(start, stop, body):
        def step(index, carry):
            body(index)
            return carry

        lax.fori_loop(start, stop, step, 0)

    def remote(src, dst, ssem, rsem, device):
        return pltpu.make_async_remote_copy(
            src_ref=src, dst_ref=dst, send_sem=ssem, recv_sem=rsem,
            device_id=device, device_id_type=MESH,
        )

    tokens = (ft, bt, bc)
    route_of = (0, 1, 1)

    def own_block(q):
        return pltpu.make_async_copy(tokens[q], gathered.at[q, pl.ds(j * tok, tok)], lsem.at[q])

    load_up = pltpu.make_async_copy(wu_hbm, wu, lsem.at[3])
    load_down = pltpu.make_async_copy(wd_hbm, wd, lsem.at[4])
    for q in range(3):
        own_block(q).start()
    small = tuple(
        pltpu.make_async_copy(ref, into, lsem.at[5 + at])
        for at, (ref, into) in enumerate(((fi, ids.at[0]), (fg, gates.at[0]), (bi, ids.at[1]), (bg, gates.at[1])))
    )
    for copy in small:
        copy.start()
    load_up.start()
    load_down.start()

    barrier = pltpu.get_barrier_semaphore()
    for step in range(1, side):
        pl.semaphore_signal(barrier, inc=1, device_id=gather_dev(around(j, step, side)), device_id_type=MESH)
        pl.semaphore_signal(barrier, inc=1, device_id=row_dev(around(m, step, side)), device_id_type=MESH)
    for step in range(1, nx):
        pl.semaphore_signal(barrier, inc=1, device_id=x_dev(around(x, step, nx)), device_id_type=MESH)
    pl.semaphore_signal(barrier, inc=1, device_id=core_dev, device_id_type=MESH)
    pl.semaphore_wait(barrier, 2 * (side - 1) + nx)

    def block(place):
        return pl.ds(pl.multiple_of(place * tok, tok), tok)

    GATHER = (
        (0, 1, None), (0, -1, None), (-1, 1, None), (1, -1, None),
        (-2, 1, None), (2, -1, None), (-2, 2, 0), (2, -2, 1),
    )

    def gather_copy(q, kind):
        origin, target, piece = GATHER[kind]
        place = around(j, side + origin, side)
        rows = block(place)
        if piece is not None:
            rows = pl.ds(pl.multiple_of(place * tok + piece * part, part), part)
        here = gathered.at[q, rows]
        source = tokens[q] if origin == 0 else here
        return remote(source, here, gat_s.at[q, kind], gat_r.at[q, kind], gather_dev(around(j, side + target, side)))

    def info_copy(r, k):
        there = around(j, k, side)
        return remote(
            info_own.at[r, pl.ds(there * side, side)], info_all.at[r, pl.ds(j * side, side)],
            info_s.at[r], info_r.at[r], gather_dev(there),
        )

    def info_copies(r):
        rows = pl.ds(0, (side - 1) * side)
        return remote(info_own.at[r, rows], info_all.at[r, rows], info_s.at[r], info_r.at[r], gather_dev(around(j, 1, side)))

    def rows_at(n, place):
        first, count = chunks[n]
        return pl.ds(pl.multiple_of(side * first + place * count, 16), count)

    def row_copy(q, n, k):
        there = around(m, k, side)
        return remote(
            sending.at[q, rows_at(n, there)], arrived.at[q, rows_at(n, m)],
            a2a_s.at[q, n], a2a_r.at[q, n], row_dev(there),
        )

    def most_rows(n):
        first, count = chunks[n]
        return pl.ds(side * first, (side - 1) * count)

    def row_copies(q, n):
        rows = most_rows(n)
        return remote(
            sending.at[q, rows], arrived.at[q, rows], a2a_s.at[q, n], a2a_r.at[q, n], row_dev(around(m, 1, side)),
        )

    width = ft.shape[1]
    last = len(chunks) - 1

    def reduce_spans(r):
        return ((0, half), (half, width - half)) if r else ((0, width),)

    def return_spans(r, n):
        return reduce_spans(r) if n == last else ((0, width),)

    def return_copy(r, n, h, k):
        there = around(m, k, side)
        at = pl.ds(*return_spans(r, n)[h])
        return remote(
            res.at[r, rows_at(n, there), at], returned.at[r, rows_at(n, m), at],
            ret_s.at[r, n, h], ret_r.at[r, n, h], row_dev(there),
        )

    def return_copies(r, n, h):
        rows, at = most_rows(n), pl.ds(*return_spans(r, n)[h])
        return remote(
            res.at[r, rows, at], returned.at[r, rows, at],
            ret_s.at[r, n, h], ret_r.at[r, n, h], row_dev(around(m, 1, side)),
        )

    REDUCE = (
        (1, 1, None), (-1, -1, None), (3, 1, None), (-3, -1, None),
        (4, 2, 1), (4, -2, 0), (2, 2, None), (-2, -2, None),
    )

    def reduce_copy(r, h, kind):
        owner, target, piece = REDUCE[kind]
        place = around(j, side + owner, side)
        at = pl.ds(*reduce_spans(r)[h])
        source, there = part_send.at[r, block(place), at], part_recv.at[r, kind, :, at]
        if kind >= 6:
            source = fold.at[r, kind - 6, :, at]
        if piece is not None:
            source = part_send.at[r, pl.ds(pl.multiple_of(place * tok + piece * part, part), part), at]
            there = part_recv.at[r, kind, pl.ds(piece * part, part), at]
        device = gather_dev(around(j, side + target, side))
        return remote(source, there, red_s.at[r, h, kind], red_r.at[r, h, kind], device)

    def out_copy(r, h):
        at = pl.ds(*reduce_spans(r)[h])
        return pltpu.make_async_copy(result.at[r, :, at], both_out.at[r, :, at], lsem.at[9 + r + h])

    def all_rows(n):
        first, count = chunks[n]
        return pl.ds(side * first, side * count)

    def share(n, place):
        first, count = chunks[n]
        size = side * count // nx
        return pl.ds(pl.multiple_of(side * first + place * size, 16), size)

    def pair_copy(q, n):
        return remote(
            pair_out.at[q, all_rows(n)], pair_in.at[q, all_rows(n)],
            pr1_s.at[q, n], pr1_r.at[q, n], core_dev,
        )

    def scatter_copy(q, n, k):
        there = around(x, k, nx)
        return remote(
            xsend.at[q, share(n, there)], xrecv.at[q, share(n, x)],
            xrs_s.at[q, n], xrs_r.at[q, n], x_dev(there),
        )

    def other_shares(n):
        first, count = chunks[n]
        return pl.ds(side * first, (nx - 1) * (side * count // nx))

    def scatter_copies(q, n):
        rows = other_shares(n)
        return remote(
            xsend.at[q, rows], xrecv.at[q, rows], xrs_s.at[q, n], xrs_r.at[q, n], x_dev(around(x, 1, nx)),
        )

    def spread_copy(r, n, k):
        here = act.at[r, c, share(n, x)]
        return remote(here, here, xag_s.at[r, n], xag_r.at[r, n], x_dev(around(x, k, nx)))

    def spread_copies(r, n):
        here = act.at[r, c, other_shares(n)]
        return remote(here, here, xag_s.at[r, n], xag_r.at[r, n], x_dev(around(x, 1, nx)))

    def pair_act_copy(r, n):
        here = act.at[r, c, all_rows(n)]
        return remote(here, here, pr2_s.at[r, n], pr2_r.at[r, n], core_dev)

    def start_ring(size, copy):
        loop(1, size, lambda k: copy(k).start())

    def start_gather(q):
        for kind in (0, 1):
            gather_copy(q, kind).start()

    def pass_first(q):
        for kind in (0, 1):
            gather_copy(q, kind).wait_recv()
            gather_copy(q, kind + 2).start()

    def pass_on(q):
        for kind in (2, 3):
            gather_copy(q, kind).wait_recv()
            gather_copy(q, kind + 4).start()
            gather_copy(q, kind + 2).start()

    def route_info():
        for copy in small:
            copy.wait()
        shape = (side * side, 2 * tok)
        row = lax.broadcasted_iota(jnp.int32, shape, 0)
        lane = lax.broadcasted_iota(jnp.int32, shape, 1)
        expert = (row // side) * sj + (row % side) * sm
        wide = (2 * tok, 2 * tok)
        before = lax.broadcasted_iota(jnp.int32, wide, 0)
        after = lax.broadcasted_iota(jnp.int32, wide, 1)
        earlier = jnp.where((before < after) & (after < tok), 1.0, 0.0).astype(BF16)
        for r in range(2):
            names = jnp.concatenate([ids[r], ids[r]], axis=1)
            weights = jnp.concatenate([gates[r], gates[r]], axis=1)
            named = jnp.zeros(shape, F32)
            gate = jnp.zeros(shape, F32)
            for k in range(ids.shape[1]):
                hit = names[k:k + 1, :] == expert
                named = named + jnp.where(hit, 1.0, 0.0)
                gate = gate + jnp.where(hit, weights[k:k + 1, :], 0.0)
            rank = dot(named.astype(BF16), earlier)
            slot = jnp.where(named > 0.5, rank * side + j.astype(F32), -1.0)
            info_own[r] = jnp.where(lane < tok, slot, gate)
            here = pl.ds(pl.multiple_of(j * side, side), side)
            info_all[r, here] = info_own[r, here]
            start_ring(side, functools.partial(info_copy, r))

    def build_select(r):
        info_copies(r).wait_recv()
        for b in range(side):
            here = info_all[r, b * side:(b + 1) * side, :]
            slots[0, :, b * tok:(b + 1) * tok] = here[:, :tok]
            slots[1, :, b * tok:(b + 1) * tok] = here[:, tok:]
        for n, (first, count) in enumerate(chunks):
            def body(place):
                line = lax.broadcasted_iota(jnp.int32, (count, side * tok), 0) + first
                hit = slots[0, pl.ds(place, 1), :] == line.astype(F32)
                at = rows_at(n, place)
                sel[r, at] = jnp.where(hit, 1.0, 0.0).astype(BF16)
                gsel[r, at] = jnp.where(hit, slots[1, pl.ds(place, 1), :], 0.0).astype(BF16)

            loop(0, side, body)

    def build_perm():
        for n, (first, count) in enumerate(chunks):
            def body(place):
                shape = (count, side * count)
                line = lax.broadcasted_iota(jnp.int32, shape, 0)
                lane = lax.broadcasted_iota(jnp.int32, shape, 1)
                other = line % side
                source = other * count + (line - other) + place
                perm[rows_at(n, place), :side * count] = jnp.where(source == lane, 1.0, 0.0).astype(BF16)

            loop(0, side, body)

    def permuted(n, ref, start, size):
        first, count = chunks[n]
        matrix = perm[all_rows(n), :side * count]
        return dot(matrix, ref[:, pl.ds(start, size)]).astype(BF16)

    def await_gather(q):
        own_block(q).wait()
        for kind in (4, 5, 6, 7):
            gather_copy(q, kind).wait_recv()

    def dispatch(q, n):
        r = route_of[q]

        def body(start, size):
            at = pl.ds(start, size)
            sending[q, all_rows(n), at] = dot(sel[r, all_rows(n)], gathered[q, :, at]).astype(BF16)

        column_tiles(width, tile, body)
        start_ring(side, functools.partial(row_copy, q, n))
        here = rows_at(n, m)
        arrived[q, here] = sending[q, here]

    def project(q, n):
        row_copies(q, n).wait_recv()
        rows = all_rows(n)

        def product(at, size):
            if q == 2:
                return dot(arrived[q, rows], wd[pl.ds(at, size), :], NT)
            return dot(arrived[q, rows], wu[:, pl.ds(at, size)])

        def theirs(start, size):
            at = pl.multiple_of((1 - c) * half + start, 128)
            pair_tmp[rows, pl.ds(start, size)] = product(at, size).astype(BF16)
            pair_out[q, rows, pl.ds(start, size)] = permuted(n, pair_tmp.at[rows], start, size)

        def ours(start, size):
            at = pl.multiple_of(c * half + start, 128)
            kept[q, rows, pl.ds(start, size)] = product(at, size)

        column_tiles(half, tile, theirs)
        pair_copy(q, n).start()
        column_tiles(half, tile, ours)

    def scatter(q, n):
        pair_copy(q, n).wait_recv()
        rows = all_rows(n)
        xsend[q, rows] = (kept[q, rows] + pair_in[q, rows].astype(F32)).astype(BF16)
        start_ring(nx, functools.partial(scatter_copy, q, n))

    def summed(q, n):
        scatter_copies(q, n).wait_recv()
        total = xsend[q, share(n, x)].astype(F32)
        for k in range(1, nx):
            total = total + xrecv[q, share(n, around(x, k, nx))].astype(F32)
        return total

    def activate(r, n):
        if r == 0:
            pre = summed(0, n)
            value = pre / (1.0 + jnp.exp(-pre))
        else:
            pre = summed(1, n)
            grad = summed(2, n)
            sigma = 1.0 / (1.0 + jnp.exp(-pre))
            value = grad * sigma * (1.0 + pre * (1.0 - sigma))
        act[r, c, share(n, x)] = value.astype(BF16)
        start_ring(nx, functools.partial(spread_copy, r, n))

    def share_act(r, n):
        spread_copies(r, n).wait_recv()
        pair_act_copy(r, n).start()

    def expand(r, n):
        rows = all_rows(n)

        def product(left, start, at, size):
            if r == 0:
                return dot(left, wd[pl.ds(start, half), pl.ds(at, size)])
            return dot(left, wu[pl.ds(at, size), pl.ds(start, half)], NT)

        def ours(at, size):
            start = pl.multiple_of(c * half, 128)
            res_acc[rows, pl.ds(at, size)] = product(act[r, c, rows], start, at, size)

        column_tiles(width, tile, ours)
        pair_act_copy(r, n).wait_recv()

        def reorder(start, size):
            pair_tmp[rows, pl.ds(start, size)] = permuted(n, act.at[r, 1 - c, rows], start, size)

        column_tiles(half, tile, reorder)

        def theirs(at, size):
            start = pl.multiple_of((1 - c) * half, 128)
            here = pl.ds(at, size)
            total = res_acc[rows, here] + product(pair_tmp[rows], start, at, size)
            res[r, rows, here] = total.astype(BF16)

        for h, (at, size) in enumerate(return_spans(r, n)):
            column_tiles(size, tile, lambda start, count, at=at: theirs(at + start, count))
            start_ring(side, functools.partial(return_copy, r, n, h))
        here = rows_at(n, m)
        returned[r, here] = res[r, here]

    def combine(r, n, h):
        if n == last or h == 0:
            return_copies(r, n, h).wait_recv()
        rows = all_rows(n)
        base, columns = reduce_spans(r)[h]

        def body(at, size):
            here = pl.ds(base + at, size)
            total = dot(gsel[r, rows], returned[r, rows, here], TN)
            if n:
                total = total + partial[r, :, here]
            partial[r, :, here] = total
            if n == last:
                part_send[r, :, here] = total.astype(BF16)

        column_tiles(columns, tile, body)
        if n == last:
            for kind in (4, 5, 2, 3, 0, 1):
                reduce_copy(r, h, kind).start()

    def fold_in(r, h):
        for kind in (2, 3, 4, 5):
            reduce_copy(r, h, kind).wait_recv()
        at = pl.ds(*reduce_spans(r)[h])
        for place, owner in enumerate((2, -2)):
            start = around(j, side + owner, side) * tok
            for piece in range(2):
                mine = pl.ds(pl.multiple_of(start + piece * part, part), part)
                here = pl.ds(piece * part, part)
                total = partial[r, mine, at] + part_recv[r, 2 + place, here, at].astype(F32)
                if piece == 1 - place:
                    total = total + part_recv[r, 4 + place, here, at].astype(F32)
                fold[r, place, here, at] = total.astype(BF16)
            reduce_copy(r, h, 6 + place).start()

    def finish(r, h):
        at = pl.ds(*reduce_spans(r)[h])
        total = partial[r, block(j), at]
        for kind in (0, 1, 6, 7):
            reduce_copy(r, h, kind).wait_recv()
            total = total + part_recv[r, kind, :, at].astype(F32)
        result[r, :, at] = total.astype(BF16)
        out_copy(r, h).start()

    def drain():
        for q in range(3):
            for kind in range(8):
                gather_copy(q, kind).wait_send()
            for n in range(len(chunks)):
                row_copies(q, n).wait_send()
                pair_copy(q, n).wait_send()
                scatter_copies(q, n).wait_send()
        for r in range(2):
            info_copies(r).wait_send()
            for n in range(len(chunks)):
                spread_copies(r, n).wait_send()
                pair_act_copy(r, n).wait_send()
                for h in range(len(return_spans(r, n))):
                    return_copies(r, n, h).wait_send()

    start_gather(0)
    start_gather(1)
    start_gather(2)
    route_info()
    build_perm()
    pass_first(0)
    pass_first(1)
    pass_first(2)
    build_select(0)
    pass_on(0)
    pass_on(1)
    pass_on(2)
    build_select(1)
    await_gather(0)
    dispatch(0, 0)
    dispatch(0, 1)
    await_gather(1)
    dispatch(1, 0)
    await_gather(2)
    dispatch(2, 0)
    load_up.wait()
    load_down.wait()
    project(0, 0)
    scatter(0, 0)
    dispatch(1, 1)
    project(0, 1)
    scatter(0, 1)
    dispatch(2, 1)
    activate(0, 0)
    project(1, 0)
    scatter(1, 0)
    activate(0, 1)
    share_act(0, 0)
    expand(0, 0)
    project(2, 0)
    scatter(2, 0)
    share_act(0, 1)
    expand(0, 1)
    project(1, 1)
    scatter(1, 1)
    activate(1, 0)
    project(2, 1)
    scatter(2, 1)
    share_act(1, 0)
    expand(1, 0)
    combine(0, 0, 0)
    combine(0, 1, 0)
    activate(1, 1)
    share_act(1, 1)
    expand(1, 1)
    fold_in(0, 0)
    combine(1, 0, 0)
    combine(1, 0, 1)
    combine(1, 1, 0)
    combine(1, 1, 1)
    finish(0, 0)
    fold_in(1, 0)
    fold_in(1, 1)
    drain()
    finish(1, 0)
    finish(1, 1)

    for r in range(2):
        for h in range(len(reduce_spans(r))):
            for kind in range(8):
                reduce_copy(r, h, kind).wait_send()
            out_copy(r, h).wait()


def build(mesh, capacity, chunks, tile=512):
    n_pipe, n_expert = mesh.shape["pipe"], mesh.shape["expert"]
    side, nx = math.isqrt(n_expert), n_pipe // 2

    def local(ft, fi, fg, bt, bi, bg, bc, w_up, w_down):
        tok, width = ft.shape
        top = fi.shape[1]
        ff = w_up.shape[2]
        half = ff // 2
        rows = n_expert * capacity
        count = len(chunks)
        ring = side * tok
        dma = pltpu.SemaphoreType.DMA
        vmem = pltpu.VMEM
        widest = side * max(size for _, size in chunks)
        scratch = [
            vmem((width, ff), BF16), vmem((ff, width), BF16),
            vmem((2, top, tok), jnp.int32), vmem((2, top, tok), F32),
            vmem((2, n_expert, 2 * tok), F32), vmem((2, n_expert, 2 * tok), F32),
            vmem((2, side, ring), F32),
            vmem((2, rows, ring), BF16), vmem((2, rows, ring), BF16), vmem((rows, widest), BF16),
            vmem((3, ring, width), BF16), vmem((3, rows, width), BF16), vmem((3, rows, width), BF16),
            vmem((3, rows, half), F32), vmem((rows, half), BF16),
            vmem((3, rows, half), BF16), vmem((3, rows, half), BF16),
            vmem((3, rows, half), BF16), vmem((3, rows, half), BF16),
            vmem((2, 2, rows, half), BF16),
            vmem((rows, width), F32), vmem((2, rows, width), BF16), vmem((2, rows, width), BF16),
            vmem((2, ring, width), F32), vmem((2, ring, width), BF16), vmem((2, 8, tok, width), BF16),
            vmem((2, 2, tok, width), BF16), vmem((2, tok, width), BF16),
            dma((12,)), dma((2,)), dma((2,)), dma((3, 8)), dma((3, 8)),
            dma((3, count)), dma((3, count)), dma((3, count)), dma((3, count)),
            dma((3, count)), dma((3, count)), dma((2, count)), dma((2, count)),
            dma((2, count)), dma((2, count)), dma((2, count, 2)), dma((2, count, 2)),
            dma((2, 2, 8)), dma((2, 2, 8)),
        ]
        any_spec = pl.BlockSpec(memory_space=pl.ANY)
        out = jax.ShapeDtypeStruct((2, tok, width), BF16)
        results = pl.pallas_call(
            functools.partial(kernel, side, nx, chunks, tile),
            out_shape=out,
            in_specs=[any_spec] * 9,
            out_specs=any_spec,
            scratch_shapes=scratch,
            compiler_params=pltpu.CompilerParams(
                collective_id=0, has_side_effects=True, vmem_limit_bytes=60 * 2**20
            ),
            cost_estimate=pl.CostEstimate(flops=12 * rows * width * ff, bytes_accessed=6 * width * ff, transcendentals=0),
        )(ft, fi.T, fg.T, bt, bi.T, bg.T, bc, w_up[0], w_down[0])
        return results[0], results[1]

    in_specs = (
        P("expert", "pipe"), P("expert", None), P("expert", None),
        P("expert", "pipe"), P("expert", None), P("expert", None),
        P("expert", "pipe"), P("expert", "pipe", None), P("expert", None, "pipe"),
    )
    out_specs = (P("expert", "pipe"), P("expert", "pipe"))
    return jax.shard_map(local, mesh=mesh, in_specs=in_specs, out_specs=out_specs, check_vma=False)


def solution(mesh):
    return build(mesh, 10, ((0, 48), (48, 32)))
```

```python
import functools
import math

import jax
import jax.numpy as jnp
from jax import lax
from jax.experimental import pallas as pl
from jax.experimental.pallas import tpu as pltpu
from jax.sharding import PartitionSpec as P

MESH = pl.DeviceIdType.MESH
F32 = jnp.float32
BF16 = jnp.bfloat16
NN = (((1,), (0,)), ((), ()))
NT = (((1,), (1,)), ((), ()))
TN = (((0,), (0,)), ((), ()))


def dot(left, right, dims=NN):
    return lax.dot_general(left, right, dims, preferred_element_type=F32)


def column_tiles(width, tile, body):
    whole = width // tile

    def step(index, carry):
        body(pl.multiple_of(index * tile, tile), tile)
        return carry

    if whole:
        lax.fori_loop(0, whole, step, 0)
    if width % tile:
        body(whole * tile, width % tile)


def kernel(
    side, nx, chunks, tile,
    ft, fi, fg, bt, bi, bg, bc, wu_hbm, wd_hbm,
    both_out,
    wu, wd, ids, gates, info_own, info_all, slots, sel, gsel, perm,
    gathered, sending, arrived, kept, pair_tmp, pair_out, pair_in, xsend, xrecv,
    act, res_acc, res, returned, partial, part_send, part_recv, fold, result,
    lsem, info_s, info_r, gat_s, gat_r, a2a_s, a2a_r, pr1_s, pr1_r, xrs_s, xrs_r,
    xag_s, xag_r, pr2_s, pr2_r, ret_s, ret_r, red_s, red_r,
):
    tok = ft.shape[0]
    part = tok // 2
    half = wu.shape[1] // 2
    p = lax.axis_index("pipe")
    e = lax.axis_index("expert")
    x, c = p // 2, p % 2
    y, z = e // side, e % side
    j = z + c * (y - z)
    m = y + c * (z - y)
    sj = 1 + c * (side - 1)
    sm = side - c * (side - 1)

    def around(place, step, size):
        return (place + step) % size

    def gather_dev(place):
        return (p, place * sj + m * sm)

    def row_dev(place):
        return (p, j * sj + place * sm)

    def x_dev(place):
        return (place * 2 + c, e)

    core_dev = (x * 2 + 1 - c, e)

    def loop(start, stop, body):
        def step(index, carry):
            body(index)
            return carry

        lax.fori_loop(start, stop, step, 0)

    def remote(src, dst, ssem, rsem, device):
        return pltpu.make_async_remote_copy(
            src_ref=src, dst_ref=dst, send_sem=ssem, recv_sem=rsem,
            device_id=device, device_id_type=MESH,
        )

    tokens = (ft, bt, bc)
    route_of = (0, 1, 1)

    def own_block(q):
        return pltpu.make_async_copy(tokens[q], gathered.at[q, pl.ds(j * tok, tok)], lsem.at[q])

    load_up = pltpu.make_async_copy(wu_hbm, wu, lsem.at[3])
    load_down = pltpu.make_async_copy(wd_hbm, wd, lsem.at[4])
    for q in range(3):
        own_block(q).start()
    small = tuple(
        pltpu.make_async_copy(ref, into, lsem.at[5 + at])
        for at, (ref, into) in enumerate(((fi, ids.at[0]), (fg, gates.at[0]), (bi, ids.at[1]), (bg, gates.at[1])))
    )
    for copy in small:
        copy.start()
    load_up.start()
    load_down.start()

    barrier = pltpu.get_barrier_semaphore()
    for step in range(1, side):
        pl.semaphore_signal(barrier, inc=1, device_id=gather_dev(around(j, step, side)), device_id_type=MESH)
        pl.semaphore_signal(barrier, inc=1, device_id=row_dev(around(m, step, side)), device_id_type=MESH)
    for step in range(1, nx):
        pl.semaphore_signal(barrier, inc=1, device_id=x_dev(around(x, step, nx)), device_id_type=MESH)
    pl.semaphore_signal(barrier, inc=1, device_id=core_dev, device_id_type=MESH)
    pl.semaphore_wait(barrier, 2 * (side - 1) + nx)

    def block(place):
        return pl.ds(pl.multiple_of(place * tok, tok), tok)

    GATHER = (
        (0, 1, None), (0, -1, None), (-1, 1, None), (1, -1, None),
        (-2, 1, None), (2, -1, None), (-2, 2, 0), (2, -2, 1),
    )

    LAST = 4

    def gather_copy(q, kind):
        origin, target, piece = GATHER[kind]
        place = around(j, side + origin, side)
        rows = block(place)
        if piece is not None:
            rows = pl.ds(pl.multiple_of(place * tok + piece * part, part), part)
        here = gathered.at[q, rows]
        source = tokens[q] if origin == 0 else here
        return remote(source, here, gat_s.at[q], gat_r.at[q, min(kind, LAST)], gather_dev(around(j, side + target, side)))

    def gather_copies(q, count):
        rows = gathered.at[q, pl.ds(0, count)]
        return remote(rows, rows, gat_s.at[q], gat_r.at[q, LAST], gather_dev(around(j, 1, side)))

    def info_copy(r, k):
        there = around(j, k, side)
        return remote(
            info_own.at[r, pl.ds(there * side, side)], info_all.at[r, pl.ds(j * side, side)],
            info_s.at[r], info_r.at[r], gather_dev(there),
        )

    def info_copies(r):
        rows = pl.ds(0, (side - 1) * side)
        return remote(info_own.at[r, rows], info_all.at[r, rows], info_s.at[r], info_r.at[r], gather_dev(around(j, 1, side)))

    def rows_at(n, place):
        first, count = chunks[n]
        return pl.ds(pl.multiple_of(side * first + place * count, 16), count)

    def row_copy(q, n, k):
        there = around(m, k, side)
        return remote(
            sending.at[q, rows_at(n, there)], arrived.at[q, rows_at(n, m)],
            a2a_s.at[q, n], a2a_r.at[q, n], row_dev(there),
        )

    def most_rows(n):
        first, count = chunks[n]
        return pl.ds(side * first, (side - 1) * count)

    def row_copies(q, n):
        rows = most_rows(n)
        return remote(
            sending.at[q, rows], arrived.at[q, rows], a2a_s.at[q, n], a2a_r.at[q, n], row_dev(around(m, 1, side)),
        )

    width = ft.shape[1]
    last = len(chunks) - 1

    def reduce_spans(r):
        return ((0, half), (half, width - half)) if r else ((0, width),)

    def return_spans(r, n):
        return reduce_spans(r) if n == last else ((0, width),)

    def return_copy(r, n, h, k):
        there = around(m, k, side)
        at = pl.ds(*return_spans(r, n)[h])
        return remote(
            res.at[r, rows_at(n, there), at], returned.at[r, rows_at(n, m), at],
            ret_s.at[r, n, h], ret_r.at[r, n, h], row_dev(there),
        )

    def return_copies(r, n, h):
        rows, at = most_rows(n), pl.ds(*return_spans(r, n)[h])
        return remote(
            res.at[r, rows, at], returned.at[r, rows, at],
            ret_s.at[r, n, h], ret_r.at[r, n, h], row_dev(around(m, 1, side)),
        )

    REDUCE = (
        (1, 1, None), (-1, -1, None), (3, 1, None), (-3, -1, None),
        (4, 2, 1), (4, -2, 0), (2, 2, None), (-2, -2, None),
    )

    def reduce_copy(r, h, kind):
        owner, target, piece = REDUCE[kind]
        place = around(j, side + owner, side)
        at = pl.ds(*reduce_spans(r)[h])
        source, there = part_send.at[r, block(place), at], part_recv.at[r, kind, :, at]
        if kind >= 6:
            source = fold.at[r, kind - 6, :, at]
        if piece is not None:
            source = part_send.at[r, pl.ds(pl.multiple_of(place * tok + piece * part, part), part), at]
            there = part_recv.at[r, kind, pl.ds(piece * part, part), at]
        device = gather_dev(around(j, side + target, side))
        return remote(source, there, red_s.at[r, h], red_r.at[r, h, int(2 <= kind < 6)], device)

    def reduce_copies(r, h, early, count):
        rows = part_send.at[r, pl.ds(0, count), pl.ds(*reduce_spans(r)[h])]
        return remote(rows, rows, red_s.at[r, h], red_r.at[r, h, early], gather_dev(around(j, 1, side)))

    def out_copy(r, h):
        at = pl.ds(*reduce_spans(r)[h])
        return pltpu.make_async_copy(result.at[r, :, at], both_out.at[r, :, at], lsem.at[9 + r + h])

    def all_rows(n):
        first, count = chunks[n]
        return pl.ds(side * first, side * count)

    def share(n, place):
        first, count = chunks[n]
        size = side * count // nx
        return pl.ds(pl.multiple_of(side * first + place * size, 16), size)

    def pair_copy(q, n):
        return remote(
            pair_out.at[q, all_rows(n)], pair_in.at[q, all_rows(n)],
            pr1_s.at[q, n], pr1_r.at[q, n], core_dev,
        )

    def scatter_copy(q, n, k):
        there = around(x, k, nx)
        return remote(
            xsend.at[q, share(n, there)], xrecv.at[q, share(n, x)],
            xrs_s.at[q, n], xrs_r.at[q, n], x_dev(there),
        )

    def other_shares(n):
        first, count = chunks[n]
        return pl.ds(side * first, (nx - 1) * (side * count // nx))

    def scatter_copies(q, n):
        rows = other_shares(n)
        return remote(
            xsend.at[q, rows], xrecv.at[q, rows], xrs_s.at[q, n], xrs_r.at[q, n], x_dev(around(x, 1, nx)),
        )

    def spread_copy(r, n, k):
        here = act.at[r, c, share(n, x)]
        return remote(here, here, xag_s.at[r, n], xag_r.at[r, n], x_dev(around(x, k, nx)))

    def spread_copies(r, n):
        here = act.at[r, c, other_shares(n)]
        return remote(here, here, xag_s.at[r, n], xag_r.at[r, n], x_dev(around(x, 1, nx)))

    def pair_act_copy(r, n):
        here = act.at[r, c, all_rows(n)]
        return remote(here, here, pr2_s.at[r, n], pr2_r.at[r, n], core_dev)

    def start_ring(size, copy):
        loop(1, size, lambda k: copy(k).start())

    def start_gather(q):
        for kind in (0, 1):
            gather_copy(q, kind).start()

    def pass_first(q):
        for kind in (0, 1):
            gather_copy(q, kind).wait_recv()
            gather_copy(q, kind + 2).start()

    def pass_on(q):
        for kind in (2, 3):
            gather_copy(q, kind).wait_recv()
            gather_copy(q, kind + 4).start()
            gather_copy(q, kind + 2).start()

    def route_info():
        for copy in small:
            copy.wait()
        shape = (side * side, 2 * tok)
        row = lax.broadcasted_iota(jnp.int32, shape, 0)
        lane = lax.broadcasted_iota(jnp.int32, shape, 1)
        expert = (row // side) * sj + (row % side) * sm
        wide = (2 * tok, 2 * tok)
        before = lax.broadcasted_iota(jnp.int32, wide, 0)
        after = lax.broadcasted_iota(jnp.int32, wide, 1)
        earlier = jnp.where((before < after) & (after < tok), 1.0, 0.0).astype(BF16)
        for r in range(2):
            names = jnp.concatenate([ids[r], ids[r]], axis=1)
            weights = jnp.concatenate([gates[r], gates[r]], axis=1)
            named = jnp.zeros(shape, F32)
            gate = jnp.zeros(shape, F32)
            for k in range(ids.shape[1]):
                hit = names[k:k + 1, :] == expert
                named = named + jnp.where(hit, 1.0, 0.0)
                gate = gate + jnp.where(hit, weights[k:k + 1, :], 0.0)
            rank = dot(named.astype(BF16), earlier)
            slot = jnp.where(named > 0.5, rank * side + j.astype(F32), -1.0)
            info_own[r] = jnp.where(lane < tok, slot, gate)
            here = pl.ds(pl.multiple_of(j * side, side), side)
            info_all[r, here] = info_own[r, here]
            start_ring(side, functools.partial(info_copy, r))

    def build_select(r):
        info_copies(r).wait_recv()
        for b in range(side):
            here = info_all[r, b * side:(b + 1) * side, :]
            slots[0, :, b * tok:(b + 1) * tok] = here[:, :tok]
            slots[1, :, b * tok:(b + 1) * tok] = here[:, tok:]
        for n, (first, count) in enumerate(chunks):
            def body(place):
                line = lax.broadcasted_iota(jnp.int32, (count, side * tok), 0) + first
                hit = slots[0, pl.ds(place, 1), :] == line.astype(F32)
                at = rows_at(n, place)
                sel[r, at] = jnp.where(hit, 1.0, 0.0).astype(BF16)
                gsel[r, at] = jnp.where(hit, slots[1, pl.ds(place, 1), :], 0.0).astype(BF16)

            loop(0, side, body)

    def build_perm():
        for n, (first, count) in enumerate(chunks):
            def body(place):
                shape = (count, side * count)
                line = lax.broadcasted_iota(jnp.int32, shape, 0)
                lane = lax.broadcasted_iota(jnp.int32, shape, 1)
                other = line % side
                source = other * count + (line - other) + place
                perm[rows_at(n, place), :side * count] = jnp.where(source == lane, 1.0, 0.0).astype(BF16)

            loop(0, side, body)

    def permuted(n, ref, start, size):
        first, count = chunks[n]
        matrix = perm[all_rows(n), :side * count]
        return dot(matrix, ref[:, pl.ds(start, size)]).astype(BF16)

    def await_gather(q):
        own_block(q).wait()
        gather_copies(q, 3 * tok).wait_recv()

    def dispatch(q, n):
        r = route_of[q]

        def body(start, size):
            at = pl.ds(start, size)
            sending[q, all_rows(n), at] = dot(sel[r, all_rows(n)], gathered[q, :, at]).astype(BF16)

        column_tiles(width, tile, body)
        start_ring(side, functools.partial(row_copy, q, n))
        here = rows_at(n, m)
        arrived[q, here] = sending[q, here]

    def project(q, n):
        row_copies(q, n).wait_recv()
        rows = all_rows(n)

        def product(at, size):
            if q == 2:
                return dot(arrived[q, rows], wd[pl.ds(at, size), :], NT)
            return dot(arrived[q, rows], wu[:, pl.ds(at, size)])

        def theirs(start, size):
            at = pl.multiple_of((1 - c) * half + start, 128)
            pair_tmp[rows, pl.ds(start, size)] = product(at, size).astype(BF16)
            pair_out[q, rows, pl.ds(start, size)] = permuted(n, pair_tmp.at[rows], start, size)

        def ours(start, size):
            at = pl.multiple_of(c * half + start, 128)
            kept[q, rows, pl.ds(start, size)] = product(at, size)

        column_tiles(half, tile, theirs)
        pair_copy(q, n).start()
        column_tiles(half, tile, ours)

    def scatter(q, n):
        pair_copy(q, n).wait_recv()
        rows = all_rows(n)
        xsend[q, rows] = (kept[q, rows] + pair_in[q, rows].astype(F32)).astype(BF16)
        start_ring(nx, functools.partial(scatter_copy, q, n))

    def summed(q, n):
        scatter_copies(q, n).wait_recv()
        total = xsend[q, share(n, x)].astype(F32)
        for k in range(1, nx):
            total = total + xrecv[q, share(n, around(x, k, nx))].astype(F32)
        return total

    def activate(r, n):
        if r == 0:
            pre = summed(0, n)
            value = pre / (1.0 + jnp.exp(-pre))
        else:
            pre = summed(1, n)
            grad = summed(2, n)
            sigma = 1.0 / (1.0 + jnp.exp(-pre))
            value = grad * sigma * (1.0 + pre * (1.0 - sigma))
        act[r, c, share(n, x)] = value.astype(BF16)
        start_ring(nx, functools.partial(spread_copy, r, n))

    def share_act(r, n):
        spread_copies(r, n).wait_recv()
        pair_act_copy(r, n).start()

    def expand(r, n):
        rows = all_rows(n)

        def product(left, start, at, size):
            if r == 0:
                return dot(left, wd[pl.ds(start, half), pl.ds(at, size)])
            return dot(left, wu[pl.ds(at, size), pl.ds(start, half)], NT)

        def ours(at, size):
            start = pl.multiple_of(c * half, 128)
            res_acc[rows, pl.ds(at, size)] = product(act[r, c, rows], start, at, size)

        column_tiles(width, tile, ours)
        pair_act_copy(r, n).wait_recv()

        def reorder(start, size):
            pair_tmp[rows, pl.ds(start, size)] = permuted(n, act.at[r, 1 - c, rows], start, size)

        column_tiles(half, tile, reorder)

        def theirs(at, size):
            start = pl.multiple_of((1 - c) * half, 128)
            here = pl.ds(at, size)
            total = res_acc[rows, here] + product(pair_tmp[rows], start, at, size)
            res[r, rows, here] = total.astype(BF16)

        for h, (at, size) in enumerate(return_spans(r, n)):
            column_tiles(size, tile, lambda start, count, at=at: theirs(at + start, count))
            start_ring(side, functools.partial(return_copy, r, n, h))
        here = rows_at(n, m)
        returned[r, here] = res[r, here]

    def combine(r, n, h):
        if n == last or h == 0:
            return_copies(r, n, h).wait_recv()
        rows = all_rows(n)
        base, columns = reduce_spans(r)[h]

        def body(at, size):
            here = pl.ds(base + at, size)
            total = dot(gsel[r, rows], returned[r, rows, here], TN)
            if n:
                total = total + partial[r, :, here]
            partial[r, :, here] = total
            if n == last:
                part_send[r, :, here] = total.astype(BF16)

        column_tiles(columns, tile, body)
        if n == last:
            for kind in (4, 5, 2, 3, 0, 1):
                reduce_copy(r, h, kind).start()

    def fold_in(r, h):
        reduce_copies(r, h, 1, 3 * tok).wait_recv()
        at = pl.ds(*reduce_spans(r)[h])
        for place, owner in enumerate((2, -2)):
            start = around(j, side + owner, side) * tok
            for piece in range(2):
                mine = pl.ds(pl.multiple_of(start + piece * part, part), part)
                here = pl.ds(piece * part, part)
                total = partial[r, mine, at] + part_recv[r, 2 + place, here, at].astype(F32)
                if piece == 1 - place:
                    total = total + part_recv[r, 4 + place, here, at].astype(F32)
                fold[r, place, here, at] = total.astype(BF16)
            reduce_copy(r, h, 6 + place).start()

    def finish(r, h):
        at = pl.ds(*reduce_spans(r)[h])
        total = partial[r, block(j), at]
        reduce_copies(r, h, 0, 4 * tok).wait_recv()
        for kind in (0, 1, 6, 7):
            total = total + part_recv[r, kind, :, at].astype(F32)
        result[r, :, at] = total.astype(BF16)
        out_copy(r, h).start()

    def drain():
        for q in range(3):
            gather_copies(q, 7 * tok).wait_send()
            for n in range(len(chunks)):
                row_copies(q, n).wait_send()
                pair_copy(q, n).wait_send()
                scatter_copies(q, n).wait_send()
        for r in range(2):
            info_copies(r).wait_send()
            for n in range(len(chunks)):
                spread_copies(r, n).wait_send()
                pair_act_copy(r, n).wait_send()
                for h in range(len(return_spans(r, n))):
                    return_copies(r, n, h).wait_send()

    start_gather(0)
    start_gather(1)
    start_gather(2)
    route_info()
    build_perm()
    pass_first(0)
    pass_first(1)
    pass_first(2)
    build_select(0)
    pass_on(0)
    pass_on(1)
    pass_on(2)
    build_select(1)
    await_gather(0)
    dispatch(0, 0)
    dispatch(0, 1)
    await_gather(1)
    dispatch(1, 0)
    await_gather(2)
    dispatch(2, 0)
    load_up.wait()
    load_down.wait()
    project(0, 0)
    scatter(0, 0)
    dispatch(1, 1)
    project(0, 1)
    scatter(0, 1)
    dispatch(2, 1)
    activate(0, 0)
    project(1, 0)
    scatter(1, 0)
    activate(0, 1)
    share_act(0, 0)
    expand(0, 0)
    project(2, 0)
    scatter(2, 0)
    share_act(0, 1)
    expand(0, 1)
    project(1, 1)
    activate(1, 0)
    scatter(1, 1)
    project(2, 1)
    scatter(2, 1)
    share_act(1, 0)
    expand(1, 0)
    combine(0, 0, 0)
    combine(0, 1, 0)
    activate(1, 1)
    share_act(1, 1)
    expand(1, 1)
    fold_in(0, 0)
    combine(1, 0, 0)
    combine(1, 0, 1)
    combine(1, 1, 0)
    combine(1, 1, 1)
    finish(0, 0)
    fold_in(1, 0)
    fold_in(1, 1)
    drain()
    finish(1, 0)
    finish(1, 1)

    for r in range(2):
        for h in range(len(reduce_spans(r))):
            reduce_copies(r, h, 0, 7 * tok).wait_send()
            out_copy(r, h).wait()


def build(mesh, capacity, chunks, tile=512):
    n_pipe, n_expert = mesh.shape["pipe"], mesh.shape["expert"]
    side, nx = math.isqrt(n_expert), n_pipe // 2

    def local(ft, fi, fg, bt, bi, bg, bc, w_up, w_down):
        tok, width = ft.shape
        top = fi.shape[1]
        ff = w_up.shape[2]
        half = ff // 2
        rows = n_expert * capacity
        count = len(chunks)
        ring = side * tok
        dma = pltpu.SemaphoreType.DMA
        vmem = pltpu.VMEM
        widest = side * max(size for _, size in chunks)
        scratch = [
            vmem((width, ff), BF16), vmem((ff, width), BF16),
            vmem((2, top, tok), jnp.int32), vmem((2, top, tok), F32),
            vmem((2, n_expert, 2 * tok), F32), vmem((2, n_expert, 2 * tok), F32),
            vmem((2, side, ring), F32),
            vmem((2, rows, ring), BF16), vmem((2, rows, ring), BF16), vmem((rows, widest), BF16),
            vmem((3, ring, width), BF16), vmem((3, rows, width), BF16), vmem((3, rows, width), BF16),
            vmem((3, rows, half), F32), vmem((rows, half), BF16),
            vmem((3, rows, half), BF16), vmem((3, rows, half), BF16),
            vmem((3, rows, half), BF16), vmem((3, rows, half), BF16),
            vmem((2, 2, rows, half), BF16),
            vmem((rows, width), F32), vmem((2, rows, width), BF16), vmem((2, rows, width), BF16),
            vmem((2, ring, width), F32), vmem((2, ring, width), BF16), vmem((2, 8, tok, width), BF16),
            vmem((2, 2, tok, width), BF16), vmem((2, tok, width), BF16),
            dma((12,)), dma((2,)), dma((2,)), dma((3,)), dma((3, 5)),
            dma((3, count)), dma((3, count)), dma((3, count)), dma((3, count)),
            dma((3, count)), dma((3, count)), dma((2, count)), dma((2, count)),
            dma((2, count)), dma((2, count)), dma((2, count, 2)), dma((2, count, 2)),
            dma((2, 2)), dma((2, 2, 2)),
        ]
        any_spec = pl.BlockSpec(memory_space=pl.ANY)
        out = jax.ShapeDtypeStruct((2, tok, width), BF16)
        results = pl.pallas_call(
            functools.partial(kernel, side, nx, chunks, tile),
            out_shape=out,
            in_specs=[any_spec] * 9,
            out_specs=any_spec,
            scratch_shapes=scratch,
            compiler_params=pltpu.CompilerParams(
                collective_id=0, has_side_effects=True, vmem_limit_bytes=60 * 2**20
            ),
            cost_estimate=pl.CostEstimate(flops=12 * rows * width * ff, bytes_accessed=6 * width * ff, transcendentals=0),
        )(ft, fi.T, fg.T, bt, bi.T, bg.T, bc, w_up[0], w_down[0])
        return results[0], results[1]

    in_specs = (
        P("expert", "pipe"), P("expert", None), P("expert", None),
        P("expert", "pipe"), P("expert", None), P("expert", None),
        P("expert", "pipe"), P("expert", "pipe", None), P("expert", None, "pipe"),
    )
    out_specs = (P("expert", "pipe"), P("expert", "pipe"))
    return jax.shard_map(local, mesh=mesh, in_specs=in_specs, out_specs=out_specs, check_vma=False)


def solution(mesh):
    return build(mesh, 10, ((0, 48), (48, 32)))
```

```python
import functools
import math

import jax
import jax.numpy as jnp
from jax import lax
from jax.experimental import pallas as pl
from jax.experimental.pallas import tpu as pltpu
from jax.sharding import PartitionSpec as P

MESH = pl.DeviceIdType.MESH
F32 = jnp.float32
BF16 = jnp.bfloat16
NN = (((1,), (0,)), ((), ()))
NT = (((1,), (1,)), ((), ()))
TN = (((0,), (0,)), ((), ()))


def dot(left, right, dims=NN):
    return lax.dot_general(left, right, dims, preferred_element_type=F32)


def column_tiles(width, tile, body):
    whole = width // tile

    def step(index, carry):
        body(pl.multiple_of(index * tile, tile), tile)
        return carry

    if whole:
        lax.fori_loop(0, whole, step, 0)
    if width % tile:
        body(whole * tile, width % tile)


def kernel(
    side, nx, chunks, tile,
    ft, fi, fg, bt, bi, bg, bc, wu_hbm, wd_hbm,
    both_out,
    wu, wd, ids, gates, info_own, info_all, slots, sel, gsel, perm,
    gathered, sending, arrived, kept, pair_tmp, pair_out, pair_in, xsend, xrecv,
    act, res_acc, res, returned, partial, part_send, part_recv, fold, result,
    lsem, info_s, info_r, gat_s, gat_r, a2a_s, a2a_r, pr1_s, pr1_r, xrs_s, xrs_r,
    xag_s, xag_r, pr2_s, pr2_r, ret_s, ret_r, red_s, red_r,
):
    tok = ft.shape[0]
    part = tok // 2
    half = wu.shape[1] // 2
    p = lax.axis_index("pipe")
    e = lax.axis_index("expert")
    x, c = p // 2, p % 2
    y, z = e // side, e % side
    j = z + c * (y - z)
    m = y + c * (z - y)
    sj = 1 + c * (side - 1)
    sm = side - c * (side - 1)

    def around(place, step, size):
        return (place + step) % size

    def gather_dev(place):
        return (p, place * sj + m * sm)

    def row_dev(place):
        return (p, j * sj + place * sm)

    def x_dev(place):
        return (place * 2 + c, e)

    core_dev = (x * 2 + 1 - c, e)

    def loop(start, stop, body):
        def step(index, carry):
            body(index)
            return carry

        lax.fori_loop(start, stop, step, 0)

    def remote(src, dst, ssem, rsem, device):
        return pltpu.make_async_remote_copy(
            src_ref=src, dst_ref=dst, send_sem=ssem, recv_sem=rsem,
            device_id=device, device_id_type=MESH,
        )

    tokens = (ft, bt, bc)
    route_of = (0, 1, 1)

    def own_block(q):
        return pltpu.make_async_copy(tokens[q], gathered.at[q, pl.ds(j * tok, tok)], lsem.at[q])

    load_up = pltpu.make_async_copy(wu_hbm, wu, lsem.at[3])
    load_down = pltpu.make_async_copy(wd_hbm, wd, lsem.at[4])
    for q in range(3):
        own_block(q).start()
    small = tuple(
        pltpu.make_async_copy(ref, into, lsem.at[5 + at])
        for at, (ref, into) in enumerate(((fi, ids.at[0]), (fg, gates.at[0]), (bi, ids.at[1]), (bg, gates.at[1])))
    )
    for copy in small:
        copy.start()
    load_up.start()
    load_down.start()

    barrier = pltpu.get_barrier_semaphore()
    for step in range(1, side):
        pl.semaphore_signal(barrier, inc=1, device_id=gather_dev(around(j, step, side)), device_id_type=MESH)
        pl.semaphore_signal(barrier, inc=1, device_id=row_dev(around(m, step, side)), device_id_type=MESH)
    for step in range(1, nx):
        pl.semaphore_signal(barrier, inc=1, device_id=x_dev(around(x, step, nx)), device_id_type=MESH)
    pl.semaphore_signal(barrier, inc=1, device_id=core_dev, device_id_type=MESH)
    pl.semaphore_wait(barrier, 2 * (side - 1) + nx)

    def block(place):
        return pl.ds(pl.multiple_of(place * tok, tok), tok)

    GATHER = (
        (0, 1, None), (0, -1, None), (-1, 1, None), (1, -1, None),
        (-2, 1, None), (2, -1, None), (-2, 2, 0), (2, -2, 1),
    )

    LAST = 4

    def gather_copy(q, kind):
        origin, target, piece = GATHER[kind]
        place = around(j, side + origin, side)
        rows = block(place)
        if piece is not None:
            rows = pl.ds(pl.multiple_of(place * tok + piece * part, part), part)
        here = gathered.at[q, rows]
        source = tokens[q] if origin == 0 else here
        return remote(source, here, gat_s.at[q], gat_r.at[q, min(kind, LAST)], gather_dev(around(j, side + target, side)))

    def gather_copies(q, count):
        rows = gathered.at[q, pl.ds(0, count)]
        return remote(rows, rows, gat_s.at[q], gat_r.at[q, LAST], gather_dev(around(j, 1, side)))

    def info_copy(r, k):
        there = around(j, k, side)
        return remote(
            info_own.at[r, pl.ds(there * side, side)], info_all.at[r, pl.ds(j * side, side)],
            info_s.at[r], info_r.at[r], gather_dev(there),
        )

    def info_copies(r):
        rows = pl.ds(0, (side - 1) * side)
        return remote(info_own.at[r, rows], info_all.at[r, rows], info_s.at[r], info_r.at[r], gather_dev(around(j, 1, side)))

    def rows_at(n, place):
        first, count = chunks[n]
        return pl.ds(pl.multiple_of(side * first + place * count, 16), count)

    def row_copy(q, n, k):
        there = around(m, k, side)
        return remote(
            sending.at[q, rows_at(n, there)], arrived.at[q, rows_at(n, m)],
            a2a_s.at[q, n], a2a_r.at[q, n], row_dev(there),
        )

    def most_rows(n):
        first, count = chunks[n]
        return pl.ds(side * first, (side - 1) * count)

    def row_copies(q, n):
        rows = most_rows(n)
        return remote(
            sending.at[q, rows], arrived.at[q, rows], a2a_s.at[q, n], a2a_r.at[q, n], row_dev(around(m, 1, side)),
        )

    width = ft.shape[1]
    last = len(chunks) - 1

    def reduce_spans(r):
        return ((0, half), (half, width - half)) if r else ((0, width),)

    def return_spans(r, n):
        return reduce_spans(r) if n == last else ((0, width),)

    def return_copy(r, n, h, k):
        there = around(m, k, side)
        at = pl.ds(*return_spans(r, n)[h])
        return remote(
            res.at[r, rows_at(n, there), at], returned.at[r, rows_at(n, m), at],
            ret_s.at[r, n, h], ret_r.at[r, n, h], row_dev(there),
        )

    def return_copies(r, n, h):
        rows, at = most_rows(n), pl.ds(*return_spans(r, n)[h])
        return remote(
            res.at[r, rows, at], returned.at[r, rows, at],
            ret_s.at[r, n, h], ret_r.at[r, n, h], row_dev(around(m, 1, side)),
        )

    REDUCE = (
        (1, 1, None), (-1, -1, None), (3, 1, None), (-3, -1, None),
        (4, 2, 1), (4, -2, 0), (2, 2, None), (-2, -2, None),
    )

    def reduce_copy(r, h, kind):
        owner, target, piece = REDUCE[kind]
        place = around(j, side + owner, side)
        at = pl.ds(*reduce_spans(r)[h])
        source, there = part_send.at[r, block(place), at], part_recv.at[r, kind, :, at]
        if kind >= 6:
            source = fold.at[r, kind - 6, :, at]
        if piece is not None:
            source = part_send.at[r, pl.ds(pl.multiple_of(place * tok + piece * part, part), part), at]
            there = part_recv.at[r, kind, pl.ds(piece * part, part), at]
        device = gather_dev(around(j, side + target, side))
        return remote(source, there, red_s.at[r, h], red_r.at[r, h, int(2 <= kind < 6)], device)

    def reduce_copies(r, h, early, count):
        rows = part_send.at[r, pl.ds(0, count), pl.ds(*reduce_spans(r)[h])]
        return remote(rows, rows, red_s.at[r, h], red_r.at[r, h, early], gather_dev(around(j, 1, side)))

    def out_copy(r, h):
        at = pl.ds(*reduce_spans(r)[h])
        return pltpu.make_async_copy(result.at[r, :, at], both_out.at[r, :, at], lsem.at[9 + r + h])

    def all_rows(n):
        first, count = chunks[n]
        return pl.ds(side * first, side * count)

    def share(n, place):
        first, count = chunks[n]
        size = side * count // nx
        return pl.ds(pl.multiple_of(side * first + place * size, 16), size)

    def pair_copy(q, n):
        return remote(
            pair_out.at[q, all_rows(n)], pair_in.at[q, all_rows(n)],
            pr1_s.at[q, n], pr1_r.at[q, n], core_dev,
        )

    def scatter_copy(q, n, k):
        there = around(x, k, nx)
        return remote(
            xsend.at[q, share(n, there)], xrecv.at[q, share(n, x)],
            xrs_s.at[q, n], xrs_r.at[q, n], x_dev(there),
        )

    def other_shares(n):
        first, count = chunks[n]
        return pl.ds(side * first, (nx - 1) * (side * count // nx))

    def scatter_copies(q, n):
        rows = other_shares(n)
        return remote(
            xsend.at[q, rows], xrecv.at[q, rows], xrs_s.at[q, n], xrs_r.at[q, n], x_dev(around(x, 1, nx)),
        )

    def spread_copy(r, n, k):
        here = act.at[r, c, share(n, x)]
        return remote(here, here, xag_s.at[r, n], xag_r.at[r, n], x_dev(around(x, k, nx)))

    def spread_copies(r, n):
        here = act.at[r, c, other_shares(n)]
        return remote(here, here, xag_s.at[r, n], xag_r.at[r, n], x_dev(around(x, 1, nx)))

    def pair_act_copy(r, n):
        here = act.at[r, c, all_rows(n)]
        return remote(here, here, pr2_s.at[r, n], pr2_r.at[r, n], core_dev)

    def start_ring(size, copy):
        loop(1, size, lambda k: copy(k).start())

    def start_gather(q):
        for kind in (0, 1):
            gather_copy(q, kind).start()

    def pass_first(q):
        for kind in (0, 1):
            gather_copy(q, kind).wait_recv()
            gather_copy(q, kind + 2).start()

    def pass_on(q):
        for kind in (2, 3):
            gather_copy(q, kind).wait_recv()
            gather_copy(q, kind + 4).start()
            gather_copy(q, kind + 2).start()

    def route_info():
        for copy in small:
            copy.wait()
        shape = (side * side, 2 * tok)
        row = lax.broadcasted_iota(jnp.int32, shape, 0)
        lane = lax.broadcasted_iota(jnp.int32, shape, 1)
        expert = (row // side) * sj + (row % side) * sm
        wide = (2 * tok, 2 * tok)
        before = lax.broadcasted_iota(jnp.int32, wide, 0)
        after = lax.broadcasted_iota(jnp.int32, wide, 1)
        earlier = jnp.where((before < after) & (after < tok), 1.0, 0.0).astype(BF16)
        for r in range(2):
            names = jnp.concatenate([ids[r], ids[r]], axis=1)
            weights = jnp.concatenate([gates[r], gates[r]], axis=1)
            named = jnp.zeros(shape, F32)
            gate = jnp.zeros(shape, F32)
            for k in range(ids.shape[1]):
                hit = names[k:k + 1, :] == expert
                named = named + jnp.where(hit, 1.0, 0.0)
                gate = gate + jnp.where(hit, weights[k:k + 1, :], 0.0)
            rank = dot(named.astype(BF16), earlier)
            slot = jnp.where(named > 0.5, rank * side + j.astype(F32), -1.0)
            info_own[r] = jnp.where(lane < tok, slot, gate)
            here = pl.ds(pl.multiple_of(j * side, side), side)
            info_all[r, here] = info_own[r, here]
            start_ring(side, functools.partial(info_copy, r))

    def build_select(r):
        info_copies(r).wait_recv()
        for b in range(side):
            here = info_all[r, b * side:(b + 1) * side, :]
            slots[0, :, b * tok:(b + 1) * tok] = here[:, :tok]
            slots[1, :, b * tok:(b + 1) * tok] = here[:, tok:]
        for n, (first, count) in enumerate(chunks):
            def body(place):
                line = lax.broadcasted_iota(jnp.int32, (count, side * tok), 0) + first
                hit = slots[0, pl.ds(place, 1), :] == line.astype(F32)
                at = rows_at(n, place)
                sel[r, at] = jnp.where(hit, 1.0, 0.0).astype(BF16)
                gsel[r, at] = jnp.where(hit, slots[1, pl.ds(place, 1), :], 0.0).astype(BF16)

            loop(0, side, body)

    def build_perm():
        for n, (first, count) in enumerate(chunks):
            def body(place):
                shape = (count, side * count)
                line = lax.broadcasted_iota(jnp.int32, shape, 0)
                lane = lax.broadcasted_iota(jnp.int32, shape, 1)
                other = line % side
                source = other * count + (line - other) + place
                perm[rows_at(n, place), :side * count] = jnp.where(source == lane, 1.0, 0.0).astype(BF16)

            loop(0, side, body)

    def permuted(n, ref, start, size):
        first, count = chunks[n]
        matrix = perm[all_rows(n), :side * count]
        return dot(matrix, ref[:, pl.ds(start, size)]).astype(BF16)

    def await_gather(q):
        own_block(q).wait()
        gather_copies(q, 3 * tok).wait_recv()

    def dispatch(q, n):
        r = route_of[q]

        def body(start, size):
            at = pl.ds(start, size)
            sending[q, all_rows(n), at] = dot(sel[r, all_rows(n)], gathered[q, :, at]).astype(BF16)

        column_tiles(width, tile, body)
        start_ring(side, functools.partial(row_copy, q, n))
        here = rows_at(n, m)
        arrived[q, here] = sending[q, here]

    def project(q, n):
        row_copies(q, n).wait_recv()
        rows = all_rows(n)

        def product(at, size):
            if q == 2:
                return dot(arrived[q, rows], wd[pl.ds(at, size), :], NT)
            return dot(arrived[q, rows], wu[:, pl.ds(at, size)])

        def theirs(start, size):
            at = pl.multiple_of((1 - c) * half + start, 128)
            pair_tmp[rows, pl.ds(start, size)] = product(at, size).astype(BF16)
            pair_out[q, rows, pl.ds(start, size)] = permuted(n, pair_tmp.at[rows], start, size)

        def ours(start, size):
            at = pl.multiple_of(c * half + start, 128)
            kept[q, rows, pl.ds(start, size)] = product(at, size)

        column_tiles(half, tile, theirs)
        pair_copy(q, n).start()
        column_tiles(half, tile, ours)

    def scatter(q, n):
        pair_copy(q, n).wait_recv()
        rows = all_rows(n)
        xsend[q, rows] = (kept[q, rows] + pair_in[q, rows].astype(F32)).astype(BF16)
        start_ring(nx, functools.partial(scatter_copy, q, n))

    def summed(q, n):
        scatter_copies(q, n).wait_recv()
        total = xsend[q, share(n, x)].astype(F32)
        for k in range(1, nx):
            total = total + xrecv[q, share(n, around(x, k, nx))].astype(F32)
        return total

    def activate(r, n):
        if r == 0:
            pre = summed(0, n)
            value = pre / (1.0 + jnp.exp(-pre))
        else:
            pre = summed(1, n)
            grad = summed(2, n)
            sigma = 1.0 / (1.0 + jnp.exp(-pre))
            value = grad * sigma * (1.0 + pre * (1.0 - sigma))
        act[r, c, share(n, x)] = value.astype(BF16)
        start_ring(nx, functools.partial(spread_copy, r, n))

    def share_act(r, n):
        spread_copies(r, n).wait_recv()
        pair_act_copy(r, n).start()

    def expand(r, n):
        rows = all_rows(n)

        def product(left, start, at, size):
            if r == 0:
                return dot(left, wd[pl.ds(start, half), pl.ds(at, size)])
            return dot(left, wu[pl.ds(at, size), pl.ds(start, half)], NT)

        def ours(at, size):
            start = pl.multiple_of(c * half, 128)
            res_acc[rows, pl.ds(at, size)] = product(act[r, c, rows], start, at, size)

        column_tiles(width, tile, ours)
        pair_act_copy(r, n).wait_recv()

        def reorder(start, size):
            pair_tmp[rows, pl.ds(start, size)] = permuted(n, act.at[r, 1 - c, rows], start, size)

        column_tiles(half, tile, reorder)

        def theirs(at, size):
            start = pl.multiple_of((1 - c) * half, 128)
            here = pl.ds(at, size)
            total = res_acc[rows, here] + product(pair_tmp[rows], start, at, size)
            res[r, rows, here] = total.astype(BF16)

        for h, (at, size) in enumerate(return_spans(r, n)):
            column_tiles(size, tile, lambda start, count, at=at: theirs(at + start, count))
            start_ring(side, functools.partial(return_copy, r, n, h))
        here = rows_at(n, m)
        returned[r, here] = res[r, here]

    def combine(r, n, h):
        if n == last or h == 0:
            return_copies(r, n, h).wait_recv()
        rows = all_rows(n)
        base, columns = reduce_spans(r)[h]

        def body(at, size):
            here = pl.ds(base + at, size)
            total = dot(gsel[r, rows], returned[r, rows, here], TN)
            if n:
                total = total + partial[r, :, here]
            partial[r, :, here] = total
            if n == last:
                part_send[r, :, here] = total.astype(BF16)

        column_tiles(columns, tile, body)
        if n == last:
            for kind in (4, 5, 2, 3, 0, 1):
                reduce_copy(r, h, kind).start()

    def fold_in(r, h):
        reduce_copies(r, h, 1, 3 * tok).wait_recv()
        at = pl.ds(*reduce_spans(r)[h])
        for place, owner in enumerate((2, -2)):
            start = around(j, side + owner, side) * tok
            for piece in range(2):
                mine = pl.ds(pl.multiple_of(start + piece * part, part), part)
                here = pl.ds(piece * part, part)
                total = partial[r, mine, at] + part_recv[r, 2 + place, here, at].astype(F32)
                if piece == 1 - place:
                    total = total + part_recv[r, 4 + place, here, at].astype(F32)
                fold[r, place, here, at] = total.astype(BF16)
            reduce_copy(r, h, 6 + place).start()

    def finish(r, h):
        at = pl.ds(*reduce_spans(r)[h])
        total = partial[r, block(j), at]
        reduce_copies(r, h, 0, 4 * tok).wait_recv()
        for kind in (0, 1, 6, 7):
            total = total + part_recv[r, kind, :, at].astype(F32)
        result[r, :, at] = total.astype(BF16)
        out_copy(r, h).start()

    def drain():
        for q in range(3):
            gather_copies(q, 7 * tok).wait_send()
            for n in range(len(chunks)):
                row_copies(q, n).wait_send()
                pair_copy(q, n).wait_send()
                scatter_copies(q, n).wait_send()
        for r in range(2):
            info_copies(r).wait_send()
            for n in range(len(chunks)):
                spread_copies(r, n).wait_send()
                pair_act_copy(r, n).wait_send()
                for h in range(len(return_spans(r, n))):
                    return_copies(r, n, h).wait_send()

    start_gather(0)
    start_gather(1)
    start_gather(2)
    route_info()
    build_perm()
    pass_first(0)
    pass_first(1)
    pass_first(2)
    build_select(0)
    pass_on(0)
    pass_on(1)
    pass_on(2)
    build_select(1)
    await_gather(0)
    dispatch(0, 0)
    dispatch(0, 1)
    await_gather(1)
    dispatch(1, 0)
    await_gather(2)
    dispatch(2, 0)
    load_up.wait()
    load_down.wait()
    project(0, 0)
    scatter(0, 0)
    dispatch(1, 1)
    project(0, 1)
    scatter(0, 1)
    dispatch(2, 1)
    activate(0, 0)
    project(1, 0)
    scatter(1, 0)
    activate(0, 1)
    share_act(0, 0)
    expand(0, 0)
    project(2, 0)
    scatter(2, 0)
    share_act(0, 1)
    expand(0, 1)
    project(1, 1)
    activate(1, 0)
    scatter(1, 1)
    project(2, 1)
    scatter(2, 1)
    share_act(1, 0)
    expand(1, 0)
    combine(0, 0, 0)
    combine(0, 1, 0)
    activate(1, 1)
    share_act(1, 1)
    expand(1, 1)
    fold_in(0, 0)
    combine(1, 0, 0)
    combine(1, 0, 1)
    combine(1, 1, 0)
    combine(1, 1, 1)
    finish(0, 0)
    fold_in(1, 0)
    fold_in(1, 1)
    drain()
    finish(1, 0)
    finish(1, 1)

    for r in range(2):
        for h in range(len(reduce_spans(r))):
            reduce_copies(r, h, 0, 7 * tok).wait_send()
            out_copy(r, h).wait()


def build(mesh, capacity, chunks, tile=512):
    n_pipe, n_expert = mesh.shape["pipe"], mesh.shape["expert"]
    side, nx = math.isqrt(n_expert), n_pipe // 2

    def local(ft, fi, fg, bt, bi, bg, bc, w_up, w_down):
        tok, width = ft.shape
        top = fi.shape[1]
        ff = w_up.shape[2]
        half = ff // 2
        rows = n_expert * capacity
        count = len(chunks)
        ring = side * tok
        dma = pltpu.SemaphoreType.DMA
        vmem = pltpu.VMEM
        widest = side * max(size for _, size in chunks)
        scratch = [
            vmem((width, ff), BF16), vmem((ff, width), BF16),
            vmem((2, top, tok), jnp.int32), vmem((2, top, tok), F32),
            vmem((2, n_expert, 2 * tok), F32), vmem((2, n_expert, 2 * tok), F32),
            vmem((2, side, ring), F32),
            vmem((2, rows, ring), BF16), vmem((2, rows, ring), BF16), vmem((rows, widest), BF16),
            vmem((3, ring, width), BF16), vmem((3, rows, width), BF16), vmem((3, rows, width), BF16),
            vmem((3, rows, half), F32), vmem((rows, half), BF16),
            vmem((3, rows, half), BF16), vmem((3, rows, half), BF16),
            vmem((3, rows, half), BF16), vmem((3, rows, half), BF16),
            vmem((2, 2, rows, half), BF16),
            vmem((rows, width), F32), vmem((2, rows, width), BF16), vmem((2, rows, width), BF16),
            vmem((2, ring, width), F32), vmem((2, ring, width), BF16), vmem((2, 8, tok, width), BF16),
            vmem((2, 2, tok, width), BF16), vmem((2, tok, width), BF16),
            dma((12,)), dma((2,)), dma((2,)), dma((3,)), dma((3, 5)),
            dma((3, count)), dma((3, count)), dma((3, count)), dma((3, count)),
            dma((3, count)), dma((3, count)), dma((2, count)), dma((2, count)),
            dma((2, count)), dma((2, count)), dma((2, count, 2)), dma((2, count, 2)),
            dma((2, 2)), dma((2, 2, 2)),
        ]
        any_spec = pl.BlockSpec(memory_space=pl.ANY)
        out = jax.ShapeDtypeStruct((2, tok, width), BF16)
        results = pl.pallas_call(
            functools.partial(kernel, side, nx, chunks, tile),
            out_shape=out,
            in_specs=[any_spec] * 9,
            out_specs=any_spec,
            scratch_shapes=scratch,
            compiler_params=pltpu.CompilerParams(
                collective_id=0, has_side_effects=True, vmem_limit_bytes=60 * 2**20
            ),
            cost_estimate=pl.CostEstimate(flops=12 * rows * width * ff, bytes_accessed=6 * width * ff, transcendentals=0),
        )(ft, fi.T, fg.T, bt, bi.T, bg.T, bc, w_up[0], w_down[0])
        return results[0], results[1]

    in_specs = (
        P("expert", "pipe"), P("expert", None), P("expert", None),
        P("expert", "pipe"), P("expert", None), P("expert", None),
        P("expert", "pipe"), P("expert", "pipe", None), P("expert", None, "pipe"),
    )
    out_specs = (P("expert", "pipe"), P("expert", "pipe"))
    return jax.shard_map(local, mesh=mesh, in_specs=in_specs, out_specs=out_specs, check_vma=False)


def solution(mesh):
    return build(mesh, 10, ((0, 32), (32, 48)))
```
